128 devices in a mesh: neu: 16 (over x_hi, y, core), tri: 8 (over x_lo, z).
Axes of the slice: x: 4 (x_hi: 2, x_lo: 2; x = x_hi * 2 + x_lo), y: 4, z: 4, core: 2. Of those that a mesh axis runs over, the one named last changes fastest.
Arguments:
- spike_counts: bfloat16 [128, 32768, 256], P('tri', 'neu')
- time_factor: bfloat16 [256, 128], replicated, may hold values from -6 to 6
- trial_factor: bfloat16 [128, 128], P('tri'), may hold values from -6 to 6
Outputs:
- neuron_new: float32 [32768, 128], P('neu')
- trial_new: float32 [128, 128], P('tri')
- time_new: float32 [256, 128], replicated
- weights: float32 [128], replicated
The draws below stay inside these ranges and needn't reach their ends.
All inputs are finite; a program needn't handle non-finite values.
Results may differ from the reference program's by a relative error of at most 0.0004.
Values sent between devices are 32-bit elements; how exact they have to be, the bound alone decides.
No kernel may reach another device: no remote copies, remote signals or barrier semaphores. Data moves between devices by JAX's collectives and lax.ppermute only.
A program may use at most 128 MiB of HBM per device.

```python
import math
import jax
import jax.numpy as jnp
from jax import lax

RANK = 128
TIME = 256
NEURONS = 32768
TRIALS = 128


def draw_spike_counts(key, part):
    key = jax.random.fold_in(key, 11)
    base_key, rough_key, trial_key = jax.random.split(key, 3)
    ramp = jnp.exp(math.log(3.0) * jnp.arange(NEURONS, dtype=jnp.float32) / max(NEURONS - 1, 1))
    rough = jnp.exp(jax.random.uniform(rough_key, (NEURONS,), jnp.float32, 0.0, math.log(3.4)))
    neuron_scale = ramp * rough
    trial_scale = jnp.exp(jax.random.uniform(trial_key, (TRIALS,), jnp.float32, 0.0, math.log(2.0)))
    shape = (TRIALS, NEURONS, TIME)
    base = jax.random.normal(base_key, shape, jnp.float32)
    values = base * neuron_scale[None, :, None] * trial_scale[:, None, None]
    return values.astype(jnp.bfloat16)


def levels(own_key, dims, cuts, least, top_value):
    def one(axis_at, shards_of):
        draws = jax.random.uniform(jax.random.fold_in(jax.random.fold_in(own_key, 6), axis_at), (shards_of,), jnp.float32, least / len(cuts), top_value / len(cuts))
        return jnp.repeat(jnp.exp(draws), dims[axis_at] // shards_of).reshape((-1,) + (1,) * (len(dims) - axis_at - 1))

    level = one(*cuts[0])
    for cut in cuts[1:]:
        level = level * one(*cut)
    return level


def scatter_about(own_key, extent, width, limit, cuts=(), kind=jnp.bfloat16):
    loudness = levels(own_key, extent, cuts, -0.22, 0.18) if cuts else 1.0
    entries = jax.random.normal(own_key, extent, jnp.float32) * width * loudness
    return jnp.minimum(jnp.maximum(entries, -limit), limit).astype(kind)


def setup_inputs(seed: int = 0) -> dict:
    key_list = jax.random.split(jax.random.key(seed), 4)
    spike_counts = draw_spike_counts(jax.random.fold_in(key_list[3], 71), 0)
    time_factor = scatter_about(key_list[1], (TIME, RANK), 1.0, 6.0)
    trial_factor = scatter_about(key_list[2], (TRIALS, RANK), 1.0, 6.0, ((0, 8),))
    return {"spike_counts": spike_counts, "time_factor": time_factor, "trial_factor": trial_factor}


highest = lax.Precision.HIGHEST

def solve_right(rhs, system):
    lower = jnp.linalg.cholesky(system)
    return jax.scipy.linalg.cho_solve((lower, True), rhs.T).T

def normalize(raw, count):
    gram_raw = jnp.dot(raw.T.astype(jnp.float32), raw.astype(jnp.float32), precision=highest, preferred_element_type=jnp.float32)
    scales = jnp.sqrt(jnp.diagonal(gram_raw) / count + 1e-06)
    return (raw / scales[None, :], gram_raw / (scales[:, None] * scales[None, :]))

def reference(spike_counts, time_factor, trial_factor):
    gram_time = jnp.dot(time_factor.T.astype(jnp.float32), time_factor.astype(jnp.float32), preferred_element_type=jnp.float32)
    gram_trial = jnp.dot(trial_factor.T.astype(jnp.float32), trial_factor.astype(jnp.float32), preferred_element_type=jnp.float32)

    def neuron_step(total, pair):
        slab, trial_row = pair
        projected = jnp.dot(slab.astype(jnp.float32), time_factor.astype(jnp.float32), preferred_element_type=jnp.float32)
        return (total + projected * trial_row.astype(jnp.float32)[None, :], None)
    start = jnp.zeros((NEURONS, RANK), jnp.float32)
    mttkrp_neuron = lax.scan(neuron_step, start, (spike_counts, trial_factor))[0]
    neuron_raw = solve_right(mttkrp_neuron, gram_time * gram_trial)
    neuron_new, gram_neuron = normalize(neuron_raw, NEURONS)
    neuron_half = neuron_new.astype(jnp.bfloat16).astype(jnp.float32)

    def trial_row_of(slab):
        projected = jnp.dot(slab.astype(jnp.float32), time_factor.astype(jnp.float32), preferred_element_type=jnp.float32)
        return lax.optimization_barrier(jnp.sum(projected * neuron_half, axis=0))
    mttkrp_trial = lax.map(trial_row_of, spike_counts)
    trial_raw = solve_right(mttkrp_trial, gram_time * gram_neuron)
    trial_new, gram_trial_new = normalize(trial_raw, TRIALS)

    def time_step(total, pair):
        slab, trial_row = pair
        khatri = (neuron_new * trial_row[None, :]).astype(jnp.bfloat16)
        return (total + jnp.dot(slab.T.astype(jnp.float32), khatri.astype(jnp.float32), preferred_element_type=jnp.float32), None)
    start_time = jnp.zeros((TIME, RANK), jnp.float32)
    mttkrp_time = lax.scan(time_step, start_time, (spike_counts, trial_new))[0]
    time_raw = solve_right(mttkrp_time, gram_neuron * gram_trial_new)
    weights = jnp.sqrt(lax.optimization_barrier(jnp.mean(time_raw * time_raw, axis=0)) + 1e-06)
    time_new = time_raw / weights[None, :]
    return (neuron_new, trial_new, time_new, weights)
```

```python
import jax
import jax.numpy as jnp
from jax import lax
from jax.experimental import pallas as pl
from jax.experimental.pallas import tpu as pltpu
from jax.sharding import PartitionSpec as P

f32 = jnp.float32
bf16 = jnp.bfloat16
highest = lax.Precision.HIGHEST
WHOLE = pl.BlockSpec(memory_space=pltpu.VMEM)
MIB = 1 << 20
AHEAD = 3


def call(kernel, outs, name, in_specs, limit=12, scratch=()):
    return pl.pallas_call(
        kernel,
        in_specs=in_specs,
        out_specs=[WHOLE] * len(outs),
        out_shape=outs,
        scratch_shapes=scratch,
        compiler_params=pltpu.CompilerParams(vmem_limit_bytes=limit * MIB),
        name=name,
    )


def array(*shape):
    return jax.ShapeDtypeStruct(shape, f32)


def dot(a, b, dims=((1,), (0,))):
    return lax.dot_general(a, b, (dims, ((), ())), precision=highest, preferred_element_type=f32)


def identity(n):
    rows = lax.broadcasted_iota(jnp.int32, (n, n), 0)
    columns = lax.broadcasted_iota(jnp.int32, (n, n), 1)
    return jnp.where(rows == columns, 1.0, 0.0).astype(f32)


def row_norm(matrix):
    return jnp.max(jnp.sum(jnp.abs(matrix), axis=1, keepdims=True))


def inverse(system, scaled_ref, approx_ref, error_ref):
    n = system.shape[0]
    eye = identity(n)
    diagonal = system * eye
    left = 1.0 / jnp.sqrt(jnp.sum(diagonal, axis=1, keepdims=True))
    right = 1.0 / jnp.sqrt(jnp.sum(diagonal, axis=0, keepdims=True))
    scaled = system * left * right
    bound = row_norm(scaled)
    step = jnp.where(bound < 1.98, 1.0, 1.96 / bound)
    error = eye - step * scaled
    scaled_ref[...] = scaled
    approx_ref[...] = step * (eye + error)
    error = dot(error, error)
    error_ref[...] = error

    def going(state):
        count, norm = state
        return (norm > 1e-2) & (count < 40)

    def square(state):
        error = error_ref[...]
        approx = approx_ref[...]
        approx_ref[...] = approx + dot(approx, error)
        error = dot(error, error)
        error_ref[...] = error
        return state[0] + 1, row_norm(error)

    lax.while_loop(going, square, (0, row_norm(error)))

    def refining(state):
        count, norm = state
        return (norm > 5e-4) & (count < 6)

    def refine(state):
        approx = approx_ref[...]
        residual = eye - dot(scaled_ref[...], approx)
        approx_ref[...] = approx + dot(approx, residual)
        return state[0] + 1, row_norm(residual)

    lax.while_loop(refining, refine, (0, jnp.float32(1.0)))
    approx = approx_ref[...]
    return approx * left * right


def neuron_pass(spikes_hbm, time_ref, trial_ref, spikes_ref, projected_ref, part_ref, sems):
    trials = spikes_ref.shape[0]
    blocks, extended, _ = part_ref.shape
    rows = extended - trials
    trial = trial_ref[...].astype(f32)
    copies = []
    for b in range(blocks):
        span = pl.ds(b * rows, rows)
        copies.append(
            pltpu.make_async_copy(spikes_hbm.at[:, span, :], spikes_ref.at[:, span, :], sems.at[b])
        )
    for b in range(min(AHEAD, blocks)):
        copies[b].start()
    for b in range(blocks):
        copies[b].wait()
        if b + AHEAD < blocks:
            copies[b + AHEAD].start()
        span = pl.ds(b * rows, rows)
        total = None
        for k in range(trials):
            projected = jnp.dot(spikes_ref[k, span, :], time_ref[...], preferred_element_type=f32)
            projected_ref[k, span, :] = projected
            term = projected * trial[k : k + 1, :]
            total = term if total is None else total + term
        part_ref[b, 0:rows, :] = total
        part_ref[b, rows:extended, :] = trial


def sum_blocks(parts_ref, copies_ref, trial_ref):
    blocks, rows, _ = copies_ref.shape
    extended = parts_ref.shape[1]
    trials = extended - rows
    total = parts_ref[0, 0:rows, :]
    for b in range(1, blocks):
        total = total + parts_ref[b, 0:rows, :]
    for b in range(blocks):
        copies_ref[b] = total
        trial_ref[b * trials : (b + 1) * trials, :] = parts_ref[b, rows:extended, :]


def first_system(time_ref, trial_ref, inverse_ref, gram_time_ref, *work):
    across = (((0,), (0,)), ((), ()))
    trial = trial_ref[...].astype(bf16)
    gram_time = lax.dot_general(time_ref[...], time_ref[...], across, preferred_element_type=f32)
    gram_trial = lax.dot_general(trial, trial, across, preferred_element_type=f32)
    gram_time_ref[...] = gram_time
    inverse_ref[...] = inverse(gram_time * gram_trial, *work)


def neuron_solve(mttkrp_ref, inverse_ref, raw_ref, gram_ref):
    raw = dot(mttkrp_ref[...], inverse_ref[...])
    raw_ref[...] = raw
    gram_ref[...] = dot(raw, raw, ((0,), (0,)))


def trial_pass(count, grams_ref, raw_ref, projected_ref, new_ref, flipped_ref, gram_ref, part_ref, half_ref):
    trials, rows, components = projected_ref.shape
    gram_raw = jnp.sum(grams_ref[...], axis=0)
    diagonal = gram_raw * identity(components)
    scale = jnp.sqrt(jnp.sum(diagonal, axis=0, keepdims=True) / count + 1e-06)
    scale_down = jnp.sqrt(jnp.sum(diagonal, axis=1, keepdims=True) / count + 1e-06)
    gram_ref[...] = gram_raw / (scale * scale_down)
    new = raw_ref[...] / scale
    new_ref[...] = new
    flipped_ref[...] = new.T
    half_ref[...] = new.astype(bf16).astype(f32)
    block = 64

    def step(b, totals):
        span = pl.ds(pl.multiple_of(b * block, block), block)
        half = half_ref[span, :]
        return [
            totals[k]
            + jnp.sum((projected_ref[k, span, :] * half).reshape(block // 8, 8, components), axis=0)
            for k in range(trials)
        ]

    totals = lax.fori_loop(0, rows // block, step, [jnp.zeros((8, components), f32)] * trials)
    part = jnp.concatenate([jnp.sum(total, axis=0, keepdims=True) for total in totals], axis=0)
    for d in range(part_ref.shape[0]):
        part_ref[d] = part


def second_system(gram_time_ref, gram_ref, inverse_ref, *work):
    inverse_ref[...] = inverse(gram_time_ref[...] * gram_ref[...], *work)


def time_pass(
    here_ref, ours_ref, theirs_ref, inverse_ref, gram_neuron_ref, flipped_ref, spikes_ref,
    trial_ref, system_ref, part_ref, table_ref,
):
    trials, rows, bins = spikes_ref.shape
    components = inverse_ref.shape[0]
    raw = dot(ours_ref[...] + theirs_ref[...], inverse_ref[...])
    gram_raw = dot(raw, raw, ((0,), (0,)))
    diagonal = gram_raw * identity(components)
    count = raw.shape[0]
    scale = jnp.sqrt(jnp.sum(diagonal, axis=0, keepdims=True) / count + 1e-06)
    scale_down = jnp.sqrt(jnp.sum(diagonal, axis=1, keepdims=True) / count + 1e-06)
    system_ref[...] = gram_neuron_ref[...] * (gram_raw / (scale * scale_down))
    table_ref[...] = raw / scale
    own = table_ref[pl.ds(pl.multiple_of(here_ref[0] * trials, trials), trials), :]
    trial_ref[...] = own
    columns = own.T
    total = None
    for k in range(trials):
        khatri_rao = (flipped_ref[...] * columns[:, k : k + 1]).astype(bf16)
        term = jnp.dot(khatri_rao, spikes_ref[k], preferred_element_type=f32)
        total = term if total is None else total + term
    part_ref[...] = total


def third_system(system_ref, inverse_ref, *work):
    inverse_ref[...] = inverse(system_ref[...], *work)


def time_solve(mttkrp_ref, inverse_ref, time_ref, weights_ref):
    raw = dot(inverse_ref[...], mttkrp_ref[...]).T
    weights = jnp.sqrt(jnp.mean(raw * raw, axis=0, keepdims=True) + 1e-06)
    weights_ref[...] = weights
    time_ref[...] = raw / weights


def body(spike_counts, time_factor, trial_factor):
    trials, rows, bins = spike_counts.shape
    components = time_factor.shape[1]
    neu, tri = lax.axis_size("neu"), lax.axis_size("tri")
    block = rows // tri
    half = neu // 2
    both = ("neu", "tri")
    swap = [(i, i ^ 1) for i in range(neu)]
    any_memory = pl.BlockSpec(memory_space=pl.ANY)

    spikes, projected, part = call(
        neuron_pass,
        [
            pltpu.VMEM(spike_counts.shape, bf16),
            pltpu.VMEM((trials, rows, components), f32),
            array(tri, block + trials, components),
        ],
        "neuron_pass",
        [any_memory, WHOLE, WHOLE],
        16,
        [pltpu.SemaphoreType.DMA((tri,))],
    )(spike_counts, time_factor, trial_factor)
    parts = lax.all_to_all(part, "tri", 0, 0)
    copies, trial_old = call(
        sum_blocks, [array(tri, block, components), array(tri * trials, components)], "sum_blocks", [WHOLE]
    )(parts)
    mttkrp_neuron = lax.all_to_all(copies, "tri", 0, 0).reshape(rows, components)
    square = array(components, components)
    work = [pltpu.VMEM((components, components), f32)] * 3
    inverse_one, gram_time = call(first_system, [square, square], "first_system", [WHOLE] * 2, 12, work)(
        time_factor, trial_old
    )
    raw, gram_part = call(neuron_solve, [array(rows, components), square], "neuron_solve", [WHOLE] * 2)(
        mttkrp_neuron, inverse_one
    )
    gram_part = gram_part + lax.ppermute(gram_part, "neu", swap)
    groups = [list(range(c, neu, 2)) for c in range(2)]
    grams = lax.all_to_all(
        jnp.broadcast_to(gram_part[None], (half, components, components)), "neu", 0, 0, axis_index_groups=groups
    )
    neuron_new, flipped, gram_neuron, trial_part = call(
        lambda *refs: trial_pass(neu * rows, *refs),
        [
            array(rows, components),
            array(components, rows),
            square,
            array(half * tri, trials, components),
        ],
        "trial_pass",
        [WHOLE] * 3,
        12,
        [pltpu.VMEM((rows, components), f32)],
    )(grams, raw, projected)
    groups = [[n * tri + t for n in range(c, neu, 2) for t in range(tri)] for c in range(2)]
    gathered = lax.all_to_all(trial_part, both, 0, 0, axis_index_groups=groups)
    (inverse_two,) = call(second_system, [square], "second_system", [WHOLE] * 2, 12, work)(gram_time, gram_neuron)
    ours = jnp.sum(gathered.reshape(half, tri * trials, components), axis=0)
    theirs = lax.ppermute(ours, "neu", swap)
    here = lax.axis_index("tri").astype(jnp.int32).reshape(1)
    trial_new, system_three, time_part = call(
        time_pass,
        [array(trials, components), square, array(components, bins)],
        "time_pass",
        [pl.BlockSpec(memory_space=pltpu.SMEM)] + [WHOLE] * 6,
        12,
        [pltpu.VMEM((tri * trials, components), f32)],
    )(here, ours, theirs, inverse_two, gram_neuron, flipped, spikes)
    pieces = lax.all_to_all(time_part.reshape(neu * tri, components // (neu * tri), bins), both, 0, 0)
    (inverse_three,) = call(third_system, [square], "third_system", [WHOLE], 12, work)(system_three)
    piece = jnp.sum(pieces, axis=0, keepdims=True)
    mttkrp_time = lax.all_to_all(jnp.broadcast_to(piece, pieces.shape), both, 0, 0).reshape(components, bins)
    time_new, weights = call(time_solve, [array(bins, components), array(1, components)], "time_solve", [WHOLE] * 2)(
        mttkrp_time, inverse_three
    )
    return neuron_new, trial_new, time_new, weights[0]


def solution(mesh):
    return jax.shard_map(
        body,
        mesh=mesh,
        in_specs=(P("tri", "neu", None), P(), P("tri", None)),
        out_specs=(P("neu", None), P("tri", None), P(), P()),
        check_vma=False,
    )
```

```python
import jax
import jax.numpy as jnp
from jax import lax
from jax.experimental import pallas as pl
from jax.experimental.pallas import tpu as pltpu
from jax.sharding import PartitionSpec as P

LIM1 = 12
f32 = jnp.float32
bf16 = jnp.bfloat16
highest = lax.Precision.HIGHEST
WHOLE = pl.BlockSpec(memory_space=pltpu.VMEM)
MIB = 1 << 20
AHEAD = 3
PAD = 8


def call(kernel, outs, name, in_specs, limit=4, scratch=()):
    return pl.pallas_call(
        kernel,
        in_specs=in_specs,
        out_specs=[WHOLE] * len(outs),
        out_shape=outs,
        scratch_shapes=scratch,
        compiler_params=pltpu.CompilerParams(vmem_limit_bytes=limit * MIB),
        name=name,
    )


def array(*shape):
    return jax.ShapeDtypeStruct(shape, f32)


def dot(a, b, dims=((1,), (0,))):
    return lax.dot_general(a, b, (dims, ((), ())), precision=highest, preferred_element_type=f32)


def identity(n):
    rows = lax.broadcasted_iota(jnp.int32, (n, n), 0)
    columns = lax.broadcasted_iota(jnp.int32, (n, n), 1)
    return jnp.where(rows == columns, 1.0, 0.0).astype(f32)


def row_norm(matrix):
    return jnp.max(jnp.sum(jnp.abs(matrix), axis=1, keepdims=True))


def inverse(system, scaled_ref, approx_ref, error_ref):
    n = system.shape[0]
    eye = identity(n)
    diagonal = system * eye
    left = 1.0 / jnp.sqrt(jnp.sum(diagonal, axis=1, keepdims=True))
    right = 1.0 / jnp.sqrt(jnp.sum(diagonal, axis=0, keepdims=True))
    scaled = system * left * right
    bound = row_norm(scaled)
    step = jnp.where(bound < 1.98, 1.0, 1.96 / bound)
    error = eye - step * scaled
    scaled_ref[...] = scaled
    approx_ref[...] = step * (eye + error)
    error = dot(error, error)
    error_ref[...] = error

    def going(state):
        count, norm = state
        return (norm > 1e-2) & (count < 40)

    def square(state):
        error = error_ref[...]
        approx = approx_ref[...]
        approx_ref[...] = approx + dot(approx, error)
        error = dot(error, error)
        error_ref[...] = error
        return state[0] + 1, row_norm(error)

    lax.while_loop(going, square, (0, row_norm(error)))

    def refining(state):
        count, norm = state
        return (norm > 5e-4) & (count < 6)

    def refine(state):
        approx = approx_ref[...]
        residual = eye - dot(scaled_ref[...], approx)
        approx_ref[...] = approx + dot(approx, residual)
        return state[0] + 1, row_norm(residual)

    lax.while_loop(refining, refine, (0, jnp.float32(1.0)))
    approx = approx_ref[...]
    return approx * left * right


def neuron_pass(spikes_hbm, time_hbm, trial_hbm, spikes_ref, projected_ref, part_ref, time_ref, trial_ref, sems):
    trials = projected_ref.shape[0]
    blocks, extended, _ = part_ref.shape
    rows = extended - trials
    small = [
        pltpu.make_async_copy(time_hbm, time_ref, sems.at[blocks]),
        pltpu.make_async_copy(trial_hbm, trial_ref, sems.at[blocks + 1]),
    ]
    for copy in small:
        copy.start()
    copies = []
    for b in range(blocks):
        span = pl.ds(b * rows, rows)
        copies.append(
            pltpu.make_async_copy(spikes_hbm.at[:, span, :], spikes_ref.at[:, span, :], sems.at[b])
        )
    for b in range(min(AHEAD, blocks)):
        copies[b].start()
    for copy in small:
        copy.wait()
    trial = trial_ref[...].astype(f32)
    for b in range(blocks):
        copies[b].wait()
        if b + AHEAD < blocks:
            copies[b + AHEAD].start()
        span = pl.ds(b * rows, rows)
        total = None
        for k in range(trials):
            projected = jnp.dot(spikes_ref[k, span, :], time_ref[...], preferred_element_type=f32)
            projected_ref[k, span, :] = projected
            term = projected * trial[k : k + 1, :]
            total = term if total is None else total + term
        part_ref[b, 0:rows, :] = total
        part_ref[b, rows:extended, :] = trial


def neuron_solve(parts_ref, time_ref, held_ref, kept_ref, copies_ref, gram_time_ref, trial_ref, *work):
    blocks, rows, _ = copies_ref.shape
    extended = parts_ref.shape[1]
    trials = extended - rows
    total = parts_ref[0, 0:rows, :]
    for b in range(1, blocks):
        total = total + parts_ref[b, 0:rows, :]
    for b in range(blocks):
        trial_ref[b * trials : (b + 1) * trials, :] = parts_ref[b, rows:extended, :].astype(bf16)
    across = (((0,), (0,)), ((), ()))
    gram_time = lax.dot_general(time_ref[...], time_ref[...], across, preferred_element_type=f32)
    gram_trial = lax.dot_general(trial_ref[...], trial_ref[...], across, preferred_element_type=f32)
    gram_time_ref[...] = gram_time
    raw = dot(total, inverse(gram_time * gram_trial, *work))
    for b in range(blocks):
        copies_ref[b] = raw


def pack_gram(ours_ref, theirs_ref, packed_ref):
    blocks, extended, components = packed_ref.shape
    rows = components // blocks
    gram = ours_ref[...] + theirs_ref[...]
    diagonal = jnp.sum(gram * identity(components), axis=0, keepdims=True)
    for d in range(blocks):
        packed_ref[d, 0:rows, :] = gram[d * rows : (d + 1) * rows, :]
        packed_ref[d, rows:extended, :] = jnp.broadcast_to(diagonal, (extended - rows, components))


def neuron_gram(raw_ref, held_ref, kept_ref, gram_ref):
    components = raw_ref.shape[1]
    raw = raw_ref[...]
    upper = raw.astype(bf16)
    lower = (raw - upper.astype(f32)).astype(bf16)
    split = jnp.concatenate([upper, lower], axis=1)
    full = lax.dot_general(split, split, (((0,), (0,)), ((), ())), preferred_element_type=f32)
    gram_ref[...] = (
        full[:components, :components]
        + (full[:components, components:] + full[components:, :components])
        + full[components:, components:]
    )


def trial_pass(count, grams_ref, raw_ref, projected_ref, kept_ref, new_ref, flipped_ref, part_ref, half_ref):
    trials, rows, components = projected_ref.shape
    tri = lax.axis_size("tri")
    gram = jnp.sum(grams_ref[...], axis=0)
    lines = components // grams_ref.shape[0]
    scale = jnp.sqrt(gram[lines : lines + 1, :] / count + 1e-06)
    share = lines // tri
    first = lax.axis_index("tri") * share
    place = lax.broadcasted_iota(jnp.int32, (lines, components), 0)
    spot = lax.broadcasted_iota(jnp.int32, (PAD, components), 0)
    sent = jnp.zeros((PAD, components), f32)
    for i in range(share):
        line = jnp.sum(jnp.where(place == first + i, gram[0:lines, :], 0.0), axis=0, keepdims=True)
        sent = jnp.where(spot == i, line, sent)
    new = raw_ref[...] / scale
    new_ref[...] = new
    flipped_ref[...] = new.T
    half_ref[...] = new.astype(bf16).astype(f32)
    block = 64

    def step(b, totals):
        span = pl.ds(pl.multiple_of(b * block, block), block)
        half = half_ref[span, :]
        return [
            totals[k]
            + jnp.sum((projected_ref[k, span, :] * half).reshape(block // 8, 8, components), axis=0)
            for k in range(trials)
        ]

    totals = lax.fori_loop(0, rows // block, step, [jnp.zeros((8, components), f32)] * trials)
    part = jnp.concatenate([jnp.sum(total, axis=0, keepdims=True) for total in totals], axis=0)
    for d in range(part_ref.shape[0]):
        part_ref[d, 0:trials, :] = part
        part_ref[d, trials:, :] = sent


def trial_sum(gathered_ref, kept_ref, sum_ref):
    tri = lax.axis_size("tri")
    chips = gathered_ref.shape[0]
    trials = gathered_ref.shape[1] - PAD
    for t in range(tri):
        total = gathered_ref[t, 0:trials, :]
        for d in range(t + tri, chips, tri):
            total = total + gathered_ref[d, 0:trials, :]
        sum_ref[t * trials : (t + 1) * trials, :] = total


def second_system(count, gram_time_ref, gathered_ref, kept_ref, inverse_ref, gram_ref, *work):
    components = gram_ref.shape[0]
    chips = gathered_ref.shape[0]
    trials = gathered_ref.shape[1] - PAD
    share = components // chips
    for d in range(chips):
        gram_ref[d * share : (d + 1) * share, :] = gathered_ref[d, trials : trials + share, :]
    gram_raw = gram_ref[...]
    diagonal = gram_raw * identity(components)
    scale = jnp.sqrt(jnp.sum(diagonal, axis=0, keepdims=True) / count + 1e-06)
    scale_down = jnp.sqrt(jnp.sum(diagonal, axis=1, keepdims=True) / count + 1e-06)
    gram = gram_raw / (scale * scale_down)
    gram_ref[...] = gram
    inverse_ref[...] = inverse(gram_time_ref[...] * gram, *work)


def time_pass(
    ours_ref, theirs_ref, inverse_ref, gram_neuron_ref, flipped_ref, spikes_ref,
    trial_ref, system_ref, part_ref, table_ref,
):
    trials, rows, bins = spikes_ref.shape
    components = inverse_ref.shape[0]
    raw = dot(ours_ref[...] + theirs_ref[...], inverse_ref[...])
    gram_raw = dot(raw, raw, ((0,), (0,)))
    diagonal = gram_raw * identity(components)
    count = raw.shape[0]
    scale = jnp.sqrt(jnp.sum(diagonal, axis=0, keepdims=True) / count + 1e-06)
    scale_down = jnp.sqrt(jnp.sum(diagonal, axis=1, keepdims=True) / count + 1e-06)
    system_ref[...] = gram_neuron_ref[...] * (gram_raw / (scale * scale_down))
    table_ref[...] = raw / scale
    own = table_ref[pl.ds(pl.multiple_of(lax.axis_index("tri") * trials, trials), trials), :]
    trial_ref[...] = own
    columns = own.T
    total = None
    for k in range(trials):
        khatri_rao = (flipped_ref[...] * columns[:, k : k + 1]).astype(bf16)
        term = jnp.dot(khatri_rao, spikes_ref[k], preferred_element_type=f32)
        total = term if total is None else total + term
    part_ref[...] = total


def third_system(system_ref, inverse_ref, *work):
    inverse_ref[...] = inverse(system_ref[...], *work)


def time_solve(mttkrp_ref, inverse_ref, time_ref, weights_ref):
    raw = dot(inverse_ref[...], mttkrp_ref[...]).T
    weights = jnp.sqrt(jnp.mean(raw * raw, axis=0, keepdims=True) + 1e-06)
    weights_ref[...] = weights
    time_ref[...] = raw / weights


def body(spike_counts, time_factor, trial_factor):
    trials, rows, bins = spike_counts.shape
    components = time_factor.shape[1]
    neu, tri = lax.axis_size("neu"), lax.axis_size("tri")
    block = rows // tri
    half = neu // 2
    both = ("neu", "tri")
    swap = [(i, i ^ 1) for i in range(neu)]
    in_hbm = pl.BlockSpec(memory_space=pltpu.HBM)

    square = array(components, components)
    work = [pltpu.VMEM((components, components), f32)] * 3

    spikes, projected, part = call(
        neuron_pass,
        [
            pltpu.VMEM(spike_counts.shape, bf16),
            pltpu.VMEM((trials, rows, components), f32),
            array(tri, block + trials, components),
        ],
        "neuron_pass",
        [in_hbm] * 3,
        LIM1,
        [
            pltpu.VMEM(time_factor.shape, bf16),
            pltpu.VMEM((trials, components), bf16),
            pltpu.SemaphoreType.DMA((tri + 2,)),
        ],
    )(spike_counts, time_factor, trial_factor)
    parts = lax.all_to_all(part, "tri", 0, 0)
    copies, gram_time = call(
        neuron_solve,
        [array(tri, block, components), square],
        "neuron_solve",
        [WHOLE] * 4,
        5,
        [pltpu.VMEM((tri * trials, components), bf16)] + work,
    )(parts, time_factor, projected, spikes)
    raw = lax.all_to_all(copies, "tri", 0, 0).reshape(rows, components)
    (gram_part,) = call(neuron_gram, [square], "neuron_gram", [WHOLE] * 3)(raw, projected, spikes)
    (packed,) = call(
        pack_gram, [array(half, components // half + PAD, components)], "pack_gram", [WHOLE] * 2
    )(gram_part, lax.ppermute(gram_part, "neu", swap))
    groups = [list(range(c, neu, 2)) for c in range(2)]
    grams = lax.all_to_all(packed, "neu", 0, 0, axis_index_groups=groups)
    neuron_new, flipped, trial_part = call(
        lambda *refs: trial_pass(neu * rows, *refs),
        [
            array(rows, components),
            array(components, rows),
            array(half * tri, trials + PAD, components),
        ],
        "trial_pass",
        [WHOLE] * 4,
        5,
        [pltpu.VMEM((rows, components), f32)],
    )(grams, raw, projected, spikes)
    groups = [[n * tri + t for n in range(c, neu, 2) for t in range(tri)] for c in range(2)]
    gathered = lax.all_to_all(trial_part, both, 0, 0, axis_index_groups=groups)
    (ours,) = call(trial_sum, [array(tri * trials, components)], "trial_sum", [WHOLE] * 2)(gathered, spikes)
    theirs = lax.ppermute(ours, "neu", swap)
    inverse_two, gram_neuron = call(
        lambda *refs: second_system(neu * rows, *refs), [square, square], "second_system", [WHOLE] * 3, 4, work
    )(gram_time, gathered, spikes)
    trial_new, system_three, time_part = call(
        time_pass,
        [array(trials, components), square, array(components, bins)],
        "time_pass",
        [WHOLE] * 6,
        5,
        [pltpu.VMEM((tri * trials, components), f32)],
    )(ours, theirs, inverse_two, gram_neuron, flipped, spikes)
    pieces = lax.all_to_all(time_part.reshape(neu * tri, components // (neu * tri), bins), both, 0, 0)
    (inverse_three,) = call(third_system, [square], "third_system", [WHOLE], 4, work)(system_three)
    piece = jnp.sum(pieces, axis=0, keepdims=True)
    mttkrp_time = lax.all_to_all(jnp.broadcast_to(piece, pieces.shape), both, 0, 0).reshape(components, bins)
    time_new, weights = call(time_solve, [array(bins, components), array(1, components)], "time_solve", [WHOLE] * 2)(
        mttkrp_time, inverse_three
    )
    return neuron_new, trial_new, time_new, weights[0]


def solution(mesh):
    return jax.shard_map(
        body,
        mesh=mesh,
        in_specs=(P("tri", "neu", None), P(), P("tri", None)),
        out_specs=(P("neu", None), P("tri", None), P(), P()),
        check_vma=False,
    )
```

```python
import jax
import jax.numpy as jnp
from jax import lax
from jax.experimental import pallas as pl
from jax.experimental.pallas import tpu as pltpu
from jax.sharding import PartitionSpec as P

LIM1 = 12
f32 = jnp.float32
bf16 = jnp.bfloat16
highest = lax.Precision.HIGHEST
WHOLE = pl.BlockSpec(memory_space=pltpu.VMEM)
MIB = 1 << 20
AHEAD = 3
PAD = 8


def call(kernel, outs, name, in_specs, limit=4, scratch=(), out_specs=None):
    return pl.pallas_call(
        kernel,
        in_specs=in_specs,
        out_specs=out_specs or [WHOLE] * len(outs),
        out_shape=outs,
        scratch_shapes=scratch,
        compiler_params=pltpu.CompilerParams(vmem_limit_bytes=limit * MIB),
        name=name,
    )


def held(value):
    return pltpu.with_memory_space_constraint(value, pltpu.VMEM)


def array(*shape):
    return jax.ShapeDtypeStruct(shape, f32)


def dot(a, b, dims=((1,), (0,))):
    return lax.dot_general(a, b, (dims, ((), ())), precision=highest, preferred_element_type=f32)


def identity(n):
    rows = lax.broadcasted_iota(jnp.int32, (n, n), 0)
    columns = lax.broadcasted_iota(jnp.int32, (n, n), 1)
    return jnp.where(rows == columns, 1.0, 0.0).astype(f32)


def row_norm(matrix):
    return jnp.max(jnp.sum(jnp.abs(matrix), axis=1, keepdims=True))


def inverse(system, scaled_ref, approx_ref, error_ref):
    n = system.shape[0]
    eye = identity(n)
    diagonal = system * eye
    left = 1.0 / jnp.sqrt(jnp.sum(diagonal, axis=1, keepdims=True))
    right = 1.0 / jnp.sqrt(jnp.sum(diagonal, axis=0, keepdims=True))
    scaled = system * left * right
    bound = row_norm(scaled)
    step = jnp.where(bound < 1.98, 1.0, 1.96 / bound)
    error = eye - step * scaled
    scaled_ref[...] = scaled
    approx_ref[...] = step * (eye + error)
    error = dot(error, error)
    error_ref[...] = error

    def going(state):
        count, norm = state
        return (norm > 1e-2) & (count < 40)

    def square(state):
        error = error_ref[...]
        approx = approx_ref[...]
        approx_ref[...] = approx + dot(approx, error)
        error = dot(error, error)
        error_ref[...] = error
        return state[0] + 1, row_norm(error)

    lax.while_loop(going, square, (0, row_norm(error)))

    def refining(state):
        count, norm = state
        return (norm > 5e-4) & (count < 6)

    def refine(state):
        approx = approx_ref[...]
        residual = eye - dot(scaled_ref[...], approx)
        approx_ref[...] = approx + dot(approx, residual)
        return state[0] + 1, row_norm(residual)

    lax.while_loop(refining, refine, (0, jnp.float32(1.0)))
    approx = approx_ref[...]
    return approx * left * right


def neuron_pass(spikes_hbm, time_hbm, trial_hbm, spikes_ref, projected_ref, part_ref, time_ref, trial_ref, sems):
    trials = projected_ref.shape[0]
    blocks, extended, _ = part_ref.shape
    rows = extended - trials
    small = [
        pltpu.make_async_copy(time_hbm, time_ref, sems.at[blocks]),
        pltpu.make_async_copy(trial_hbm, trial_ref, sems.at[blocks + 1]),
    ]
    for copy in small:
        copy.start()
    copies = []
    for b in range(blocks):
        span = pl.ds(b * rows, rows)
        copies.append(
            pltpu.make_async_copy(spikes_hbm.at[:, span, :], spikes_ref.at[:, span, :], sems.at[b])
        )
    for b in range(min(AHEAD, blocks)):
        copies[b].start()
    for copy in small:
        copy.wait()
    trial = trial_ref[...].astype(f32)
    for b in range(blocks):
        copies[b].wait()
        if b + AHEAD < blocks:
            copies[b + AHEAD].start()
        span = pl.ds(b * rows, rows)
        total = None
        for k in range(trials):
            projected = jnp.dot(spikes_ref[k, span, :], time_ref[...], preferred_element_type=f32)
            projected_ref[k, span, :] = projected
            term = projected * trial[k : k + 1, :]
            total = term if total is None else total + term
        part_ref[b, 0:rows, :] = total
        part_ref[b, rows:extended, :] = trial


def neuron_solve(parts_ref, time_ref, held_ref, kept_ref, copies_ref, gram_time_ref, trial_ref, *work):
    blocks, rows, _ = copies_ref.shape
    extended = parts_ref.shape[1]
    trials = extended - rows
    total = parts_ref[0, 0:rows, :]
    for b in range(1, blocks):
        total = total + parts_ref[b, 0:rows, :]
    for b in range(blocks):
        trial_ref[b * trials : (b + 1) * trials, :] = parts_ref[b, rows:extended, :].astype(bf16)
    across = (((0,), (0,)), ((), ()))
    gram_time = lax.dot_general(time_ref[...], time_ref[...], across, preferred_element_type=f32)
    gram_trial = lax.dot_general(trial_ref[...], trial_ref[...], across, preferred_element_type=f32)
    gram_time_ref[...] = gram_time
    raw = dot(total, inverse(gram_time * gram_trial, *work))
    for b in range(blocks):
        copies_ref[b] = raw


def pack_gram(ours_ref, theirs_ref, packed_ref):
    blocks, extended, components = packed_ref.shape
    rows = components // blocks
    gram = ours_ref[...] + theirs_ref[...]
    diagonal = jnp.sum(gram * identity(components), axis=0, keepdims=True)
    for d in range(blocks):
        packed_ref[d, 0:rows, :] = gram[d * rows : (d + 1) * rows, :]
        packed_ref[d, rows:extended, :] = jnp.broadcast_to(diagonal, (extended - rows, components))


def neuron_gram(raw_ref, held_ref, kept_ref, gram_ref):
    components = raw_ref.shape[1]
    raw = raw_ref[...]
    upper = raw.astype(bf16)
    lower = (raw - upper.astype(f32)).astype(bf16)
    split = jnp.concatenate([upper, lower], axis=1)
    full = lax.dot_general(split, split, (((0,), (0,)), ((), ())), preferred_element_type=f32)
    gram_ref[...] = (
        full[:components, :components]
        + (full[:components, components:] + full[components:, :components])
        + full[components:, components:]
    )


def trial_pass(count, grams_ref, raw_ref, projected_ref, kept_ref, new_ref, flipped_ref, part_ref, half_ref):
    trials, rows, components = projected_ref.shape
    tri = lax.axis_size("tri")
    gram = jnp.sum(grams_ref[...], axis=0)
    lines = components // grams_ref.shape[0]
    scale = jnp.sqrt(gram[lines : lines + 1, :] / count + 1e-06)
    share = lines // tri
    first = lax.axis_index("tri") * share
    place = lax.broadcasted_iota(jnp.int32, (lines, components), 0)
    spot = lax.broadcasted_iota(jnp.int32, (PAD, components), 0)
    sent = jnp.zeros((PAD, components), f32)
    for i in range(share):
        line = jnp.sum(jnp.where(place == first + i, gram[0:lines, :], 0.0), axis=0, keepdims=True)
        sent = jnp.where(spot == i, line, sent)
    new = raw_ref[...] * (1.0 / scale)
    new_ref[...] = new
    flipped_ref[...] = new.T
    half_ref[...] = new.astype(bf16).astype(f32)
    block = 64

    def step(b, totals):
        span = pl.ds(pl.multiple_of(b * block, block), block)
        half = half_ref[span, :]
        return [
            totals[k]
            + jnp.sum((projected_ref[k, span, :] * half).reshape(block // 8, 8, components), axis=0)
            for k in range(trials)
        ]

    totals = lax.fori_loop(0, rows // block, step, [jnp.zeros((8, components), f32)] * trials, unroll=2)
    part = jnp.concatenate([jnp.sum(total, axis=0, keepdims=True) for total in totals], axis=0)
    for d in range(part_ref.shape[0]):
        part_ref[d, 0:trials, :] = part
        part_ref[d, trials:, :] = sent


def trial_sum(gathered_ref, kept_ref, sum_ref):
    tri = lax.axis_size("tri")
    chips = gathered_ref.shape[0]
    trials = gathered_ref.shape[1] - PAD
    for t in range(tri):
        total = gathered_ref[t, 0:trials, :]
        for d in range(t + tri, chips, tri):
            total = total + gathered_ref[d, 0:trials, :]
        sum_ref[t * trials : (t + 1) * trials, :] = total


def second_system(count, gram_time_ref, gathered_ref, kept_ref, inverse_ref, gram_ref, *work):
    components = gram_ref.shape[0]
    chips = gathered_ref.shape[0]
    trials = gathered_ref.shape[1] - PAD
    share = components // chips
    for d in range(chips):
        gram_ref[d * share : (d + 1) * share, :] = gathered_ref[d, trials : trials + share, :]
    gram_raw = gram_ref[...]
    diagonal = gram_raw * identity(components)
    scale = jnp.sqrt(jnp.sum(diagonal, axis=0, keepdims=True) / count + 1e-06)
    scale_down = jnp.sqrt(jnp.sum(diagonal, axis=1, keepdims=True) / count + 1e-06)
    gram = gram_raw / (scale * scale_down)
    gram_ref[...] = gram
    inverse_ref[...] = inverse(gram_time_ref[...] * gram, *work)


def time_pass(
    ours_ref, theirs_ref, inverse_ref, gram_neuron_ref, flipped_ref, spikes_ref, new_ref,
    new_hbm, trial_hbm, system_hbm, part_ref, table_ref, system_ref, sems,
):
    new_copy = pltpu.make_async_copy(new_ref, new_hbm, sems.at[0])
    new_copy.start()
    trials, rows, bins = spikes_ref.shape
    components = inverse_ref.shape[0]
    raw = dot(ours_ref[...] + theirs_ref[...], inverse_ref[...])
    gram_raw = dot(raw, raw, ((0,), (0,)))
    diagonal = gram_raw * identity(components)
    count = raw.shape[0]
    scale = jnp.sqrt(jnp.sum(diagonal, axis=0, keepdims=True) / count + 1e-06)
    scale_down = jnp.sqrt(jnp.sum(diagonal, axis=1, keepdims=True) / count + 1e-06)
    system_ref[...] = gram_neuron_ref[...] * (gram_raw / (scale * scale_down))
    table_ref[...] = raw / scale
    span = pl.ds(pl.multiple_of(lax.axis_index("tri") * trials, trials), trials)
    copies = [
        pltpu.make_async_copy(table_ref.at[span, :], trial_hbm, sems.at[1]),
        pltpu.make_async_copy(system_ref, system_hbm, sems.at[2]),
    ]
    for copy in copies:
        copy.start()
    columns = table_ref[span, :].T
    total = None
    for k in range(trials):
        khatri_rao = (flipped_ref[...] * columns[:, k : k + 1]).astype(bf16)
        term = jnp.dot(khatri_rao, spikes_ref[k], preferred_element_type=f32)
        total = term if total is None else total + term
    part_ref[...] = total
    for copy in [new_copy] + copies:
        copy.wait()


def third_system(system_ref, inverse_ref, *work):
    inverse_ref[...] = inverse(system_ref[...], *work)


def time_solve(mttkrp_ref, inverse_ref, time_ref, weights_ref):
    raw = dot(inverse_ref[...], mttkrp_ref[...]).T
    weights = jnp.sqrt(jnp.mean(raw * raw, axis=0, keepdims=True) + 1e-06)
    weights_ref[...] = weights
    time_ref[...] = raw / weights


def body(spike_counts, time_factor, trial_factor):
    trials, rows, bins = spike_counts.shape
    components = time_factor.shape[1]
    neu, tri = lax.axis_size("neu"), lax.axis_size("tri")
    block = rows // tri
    half = neu // 2
    both = ("neu", "tri")
    swap = [(i, i ^ 1) for i in range(neu)]
    in_hbm = pl.BlockSpec(memory_space=pltpu.HBM)

    square = array(components, components)
    work = [pltpu.VMEM((components, components), f32)] * 3

    spikes, projected, part = call(
        neuron_pass,
        [
            pltpu.VMEM(spike_counts.shape, bf16),
            pltpu.VMEM((trials, rows, components), f32),
            array(tri, block + trials, components),
        ],
        "neuron_pass",
        [in_hbm] * 3,
        LIM1,
        [
            pltpu.VMEM(time_factor.shape, bf16),
            pltpu.VMEM((trials, components), bf16),
            pltpu.SemaphoreType.DMA((tri + 2,)),
        ],
    )(spike_counts, *[pltpu.with_memory_space_constraint(a, pltpu.HBM) for a in (time_factor, trial_factor)])
    parts = lax.all_to_all(part, "tri", 0, 0)
    copies, gram_time = call(
        neuron_solve,
        [array(tri, block, components), square],
        "neuron_solve",
        [WHOLE] * 4,
        5,
        [pltpu.VMEM((tri * trials, components), bf16)] + work,
    )(parts, time_factor, held(projected), held(spikes))
    raw = lax.all_to_all(copies, "tri", 0, 0).reshape(rows, components)
    (gram_part,) = call(neuron_gram, [square], "neuron_gram", [WHOLE] * 3)(raw, held(projected), held(spikes))
    (packed,) = call(
        pack_gram, [array(half, components // half + PAD, components)], "pack_gram", [WHOLE] * 2
    )(gram_part, lax.ppermute(gram_part, "neu", swap))
    groups = [list(range(c, neu, 2)) for c in range(2)]
    grams = lax.all_to_all(packed, "neu", 0, 0, axis_index_groups=groups)
    new, flipped, trial_part = call(
        lambda *refs: trial_pass(neu * rows, *refs),
        [
            array(rows, components),
            array(components, rows),
            array(half * tri, trials + PAD, components),
        ],
        "trial_pass",
        [WHOLE] * 4,
        5,
        [pltpu.VMEM((rows, components), f32)],
    )(grams, raw, held(projected), held(spikes))
    groups = [[n * tri + t for n in range(c, neu, 2) for t in range(tri)] for c in range(2)]
    gathered = lax.all_to_all(trial_part, both, 0, 0, axis_index_groups=groups)
    (ours,) = call(trial_sum, [array(tri * trials, components)], "trial_sum", [WHOLE] * 2)(gathered, held(spikes))
    theirs = lax.ppermute(ours, "neu", swap)
    inverse_two, gram_neuron = call(
        lambda *refs: second_system(neu * rows, *refs), [square, square], "second_system", [WHOLE] * 3, 4, work
    )(gram_time, gathered, held(spikes))
    neuron_new, trial_new, system_three, time_part = call(
        time_pass,
        [array(rows, components), array(trials, components), square, array(components, bins)],
        "time_pass",
        [WHOLE] * 7,
        5,
        [
            pltpu.VMEM((tri * trials, components), f32),
            pltpu.VMEM((components, components), f32),
            pltpu.SemaphoreType.DMA((3,)),
        ],
        [in_hbm] * 3 + [WHOLE],
    )(ours, theirs, inverse_two, gram_neuron, flipped, held(spikes), held(new))
    pieces = lax.all_to_all(time_part.reshape(neu * tri, components // (neu * tri), bins), both, 0, 0)
    (inverse_three,) = call(third_system, [square], "third_system", [WHOLE], 4, work)(system_three)
    piece = jnp.sum(pieces, axis=0, keepdims=True)
    mttkrp_time = lax.all_to_all(jnp.broadcast_to(piece, pieces.shape), both, 0, 0).reshape(components, bins)
    time_new, weights = call(time_solve, [array(bins, components), array(1, components)], "time_solve", [WHOLE] * 2)(
        mttkrp_time, inverse_three
    )
    return neuron_new, trial_new, time_new, weights[0]


def solution(mesh):
    return jax.shard_map(
        body,
        mesh=mesh,
        in_specs=(P("tri", "neu", None), P(), P("tri", None)),
        out_specs=(P("neu", None), P("tri", None), P(), P()),
        check_vma=False,
    )
```

```python
import jax
import jax.numpy as jnp
from jax import lax
from jax.experimental import pallas as pl
from jax.experimental.pallas import tpu as pltpu
from jax.sharding import PartitionSpec as P

LIM1 = 12
f32 = jnp.float32
bf16 = jnp.bfloat16
highest = lax.Precision.HIGHEST
WHOLE = pl.BlockSpec(memory_space=pltpu.VMEM)
MIB = 1 << 20
AHEAD = 3
PAD = 8


def call(kernel, outs, name, in_specs, limit=4, scratch=(), out_specs=None):
    return pl.pallas_call(
        kernel,
        in_specs=in_specs,
        out_specs=out_specs or [WHOLE] * len(outs),
        out_shape=outs,
        scratch_shapes=scratch,
        compiler_params=pltpu.CompilerParams(vmem_limit_bytes=limit * MIB),
        name=name,
    )


def held(value):
    return pltpu.with_memory_space_constraint(value, pltpu.VMEM)


def array(*shape):
    return jax.ShapeDtypeStruct(shape, f32)


def dot(a, b, dims=((1,), (0,))):
    return lax.dot_general(a, b, (dims, ((), ())), precision=highest, preferred_element_type=f32)


def rough(a, b):
    return jnp.dot(a.astype(bf16), b.astype(bf16), preferred_element_type=f32)


def fine(a, b):
    a_upper, b_upper = a.astype(bf16).astype(f32), b.astype(bf16).astype(f32)
    return rough(a_upper, b_upper) + (rough(a_upper, b - b_upper) + rough(a - a_upper, b_upper))


def identity(n):
    rows = lax.broadcasted_iota(jnp.int32, (n, n), 0)
    columns = lax.broadcasted_iota(jnp.int32, (n, n), 1)
    return jnp.where(rows == columns, 1.0, 0.0).astype(f32)


def row_norm(matrix):
    return jnp.max(jnp.sum(jnp.abs(matrix), axis=1, keepdims=True))


def inverse(system, scaled_ref, approx_ref, error_ref):
    n = system.shape[0]
    eye = identity(n)
    diagonal = system * eye
    left = 1.0 / jnp.sqrt(jnp.sum(diagonal, axis=1, keepdims=True))
    right = 1.0 / jnp.sqrt(jnp.sum(diagonal, axis=0, keepdims=True))
    scaled = system * left * right
    bound = row_norm(scaled)
    step = jnp.where(bound < 1.98, 1.0, 1.96 / bound)
    error = eye - step * scaled
    scaled_ref[...] = scaled
    approx_ref[...] = step * (eye + error)
    near = bound < 1.9

    @pl.when(near)
    def _():
        approx_ref[...] = approx_ref[...] + rough(approx_ref[...], rough(error, error))

    @pl.when(jnp.logical_not(near))
    def _():
        squared = dot(error, error)
        error_ref[...] = squared

        def going(state):
            count, norm = state
            return (norm > 1e-2) & (count < 40)

        def square(state):
            error = error_ref[...]
            approx = approx_ref[...]
            approx_ref[...] = approx + dot(approx, error)
            error = dot(error, error)
            error_ref[...] = error
            return state[0] + 1, row_norm(error)

        lax.while_loop(going, square, (0, row_norm(squared)))

    def refining(state):
        count, norm = state
        return (norm > 5e-4) & (count < 12)

    def refine(state):
        approx = approx_ref[...]
        residual = eye - dot(scaled_ref[...], approx)
        approx_ref[...] = approx + fine(approx, residual)
        return state[0] + 1, row_norm(residual)

    lax.while_loop(refining, refine, (0, jnp.float32(1.0)))
    approx = approx_ref[...]
    return approx * left * right


def neuron_pass(spikes_hbm, time_hbm, trial_hbm, spikes_ref, projected_ref, part_ref, time_ref, trial_ref, sems):
    trials = projected_ref.shape[0]
    blocks, extended, _ = part_ref.shape
    rows = extended - trials
    small = [
        pltpu.make_async_copy(time_hbm, time_ref, sems.at[blocks]),
        pltpu.make_async_copy(trial_hbm, trial_ref, sems.at[blocks + 1]),
    ]
    for copy in small:
        copy.start()
    copies = []
    for b in range(blocks):
        span = pl.ds(b * rows, rows)
        copies.append(
            pltpu.make_async_copy(spikes_hbm.at[:, span, :], spikes_ref.at[:, span, :], sems.at[b])
        )
    for b in range(min(AHEAD, blocks)):
        copies[b].start()
    for copy in small:
        copy.wait()
    trial = trial_ref[...].astype(f32)
    for b in range(blocks):
        copies[b].wait()
        if b + AHEAD < blocks:
            copies[b + AHEAD].start()
        span = pl.ds(b * rows, rows)
        total = None
        for k in range(trials):
            projected = jnp.dot(spikes_ref[k, span, :], time_ref[...], preferred_element_type=f32)
            projected_ref[k, span, :] = projected
            term = projected * trial[k : k + 1, :]
            total = term if total is None else total + term
        part_ref[b, 0:rows, :] = total
        part_ref[b, rows:extended, :] = trial


def neuron_solve(parts_ref, time_ref, held_ref, kept_ref, copies_ref, gram_time_ref, trial_ref, *work):
    blocks, rows, _ = copies_ref.shape
    extended = parts_ref.shape[1]
    trials = extended - rows
    total = parts_ref[0, 0:rows, :]
    for b in range(1, blocks):
        total = total + parts_ref[b, 0:rows, :]
    for b in range(blocks):
        trial_ref[b * trials : (b + 1) * trials, :] = parts_ref[b, rows:extended, :].astype(bf16)
    across = (((0,), (0,)), ((), ()))
    gram_time = lax.dot_general(time_ref[...], time_ref[...], across, preferred_element_type=f32)
    gram_trial = lax.dot_general(trial_ref[...], trial_ref[...], across, preferred_element_type=f32)
    gram_time_ref[...] = gram_time
    raw = dot(total, inverse(gram_time * gram_trial, *work))
    for b in range(blocks):
        copies_ref[b] = raw


def pack_gram(ours_ref, theirs_ref, packed_ref):
    blocks, extended, components = packed_ref.shape
    rows = components // blocks
    gram = ours_ref[...] + theirs_ref[...]
    diagonal = jnp.sum(gram * identity(components), axis=0, keepdims=True)
    for d in range(blocks):
        packed_ref[d, 0:rows, :] = gram[d * rows : (d + 1) * rows, :]
        packed_ref[d, rows:extended, :] = jnp.broadcast_to(diagonal, (extended - rows, components))


def neuron_gram(raw_ref, held_ref, kept_ref, gram_ref):
    components = raw_ref.shape[1]
    raw = raw_ref[...]
    upper = raw.astype(bf16)
    lower = (raw - upper.astype(f32)).astype(bf16)
    split = jnp.concatenate([upper, lower], axis=1)
    full = lax.dot_general(split, split, (((0,), (0,)), ((), ())), preferred_element_type=f32)
    gram_ref[...] = (
        full[:components, :components]
        + (full[:components, components:] + full[components:, :components])
        + full[components:, components:]
    )


def trial_pass(count, grams_ref, raw_ref, projected_ref, kept_ref, new_ref, flipped_ref, part_ref, half_ref):
    trials, rows, components = projected_ref.shape
    tri = lax.axis_size("tri")
    gram = jnp.sum(grams_ref[...], axis=0)
    lines = components // grams_ref.shape[0]
    scale = jnp.sqrt(gram[lines : lines + 1, :] / count + 1e-06)
    share = lines // tri
    first = lax.axis_index("tri") * share
    place = lax.broadcasted_iota(jnp.int32, (lines, components), 0)
    spot = lax.broadcasted_iota(jnp.int32, (PAD, components), 0)
    sent = jnp.zeros((PAD, components), f32)
    for i in range(share):
        line = jnp.sum(jnp.where(place == first + i, gram[0:lines, :], 0.0), axis=0, keepdims=True)
        sent = jnp.where(spot == i, line, sent)
    new = raw_ref[...] * (1.0 / scale)
    new_ref[...] = new
    flipped_ref[...] = new.T
    half_ref[...] = new.astype(bf16).astype(f32)
    block = 64

    def step(b, totals):
        span = pl.ds(pl.multiple_of(b * block, block), block)
        half = half_ref[span, :]
        return [
            totals[k]
            + jnp.sum((projected_ref[k, span, :] * half).reshape(block // 8, 8, components), axis=0)
            for k in range(trials)
        ]

    totals = lax.fori_loop(0, rows // block, step, [jnp.zeros((8, components), f32)] * trials, unroll=2)
    part = jnp.concatenate([jnp.sum(total, axis=0, keepdims=True) for total in totals], axis=0)
    for d in range(part_ref.shape[0]):
        part_ref[d, 0:trials, :] = part
        part_ref[d, trials:, :] = sent


def trial_sum(gathered_ref, kept_ref, sum_ref):
    tri = lax.axis_size("tri")
    chips = gathered_ref.shape[0]
    trials = gathered_ref.shape[1] - PAD
    for t in range(tri):
        total = gathered_ref[t, 0:trials, :]
        for d in range(t + tri, chips, tri):
            total = total + gathered_ref[d, 0:trials, :]
        sum_ref[t * trials : (t + 1) * trials, :] = total


def second_system(count, gram_time_ref, gathered_ref, kept_ref, inverse_ref, gram_ref, *work):
    components = gram_ref.shape[0]
    chips = gathered_ref.shape[0]
    trials = gathered_ref.shape[1] - PAD
    share = components // chips
    for d in range(chips):
        gram_ref[d * share : (d + 1) * share, :] = gathered_ref[d, trials : trials + share, :]
    gram_raw = gram_ref[...]
    diagonal = gram_raw * identity(components)
    scale = jnp.sqrt(jnp.sum(diagonal, axis=0, keepdims=True) / count + 1e-06)
    scale_down = jnp.sqrt(jnp.sum(diagonal, axis=1, keepdims=True) / count + 1e-06)
    gram = gram_raw / (scale * scale_down)
    gram_ref[...] = gram
    inverse_ref[...] = inverse(gram_time_ref[...] * gram, *work)


def time_pass(
    ours_ref, theirs_ref, inverse_ref, flipped_ref, spikes_ref, new_ref,
    new_hbm, trial_hbm, table_hbm, part_ref, table_ref, sems,
):
    new_copy = pltpu.make_async_copy(new_ref, new_hbm, sems.at[0])
    new_copy.start()
    trials, rows, bins = spikes_ref.shape
    components = inverse_ref.shape[0]
    raw = dot(ours_ref[...] + theirs_ref[...], inverse_ref[...])
    scale = jnp.sqrt(jnp.sum(raw * raw, axis=0, keepdims=True) / raw.shape[0] + 1e-06)
    table_ref[...] = raw / scale
    span = pl.ds(pl.multiple_of(lax.axis_index("tri") * trials, trials), trials)
    copies = [
        pltpu.make_async_copy(table_ref.at[span, :], trial_hbm, sems.at[1]),
        pltpu.make_async_copy(table_ref, table_hbm, sems.at[2]),
    ]
    for copy in copies:
        copy.start()
    columns = table_ref[span, :].T
    total = None
    for k in range(trials):
        khatri_rao = (flipped_ref[...] * columns[:, k : k + 1]).astype(bf16)
        term = jnp.dot(khatri_rao, spikes_ref[k], preferred_element_type=f32)
        total = term if total is None else total + term
    part_ref[...] = total
    for copy in [new_copy] + copies:
        copy.wait()


def third_system(gram_neuron_ref, table_ref, inverse_ref, *work):
    table = table_ref[...]
    inverse_ref[...] = inverse(gram_neuron_ref[...] * dot(table, table, ((0,), (0,))), *work)


def time_solve(mttkrp_ref, inverse_ref, time_ref, weights_ref):
    raw = dot(inverse_ref[...], mttkrp_ref[...]).T
    weights = jnp.sqrt(jnp.mean(raw * raw, axis=0, keepdims=True) + 1e-06)
    weights_ref[...] = weights
    time_ref[...] = raw / weights


def body(spike_counts, time_factor, trial_factor):
    trials, rows, bins = spike_counts.shape
    components = time_factor.shape[1]
    neu, tri = lax.axis_size("neu"), lax.axis_size("tri")
    block = rows // tri
    half = neu // 2
    both = ("neu", "tri")
    swap = [(i, i ^ 1) for i in range(neu)]
    in_hbm = pl.BlockSpec(memory_space=pltpu.HBM)

    square = array(components, components)
    work = [pltpu.VMEM((components, components), f32)] * 3

    spikes, projected, part = call(
        neuron_pass,
        [
            pltpu.VMEM(spike_counts.shape, bf16),
            pltpu.VMEM((trials, rows, components), f32),
            array(tri, block + trials, components),
        ],
        "neuron_pass",
        [in_hbm] * 3,
        LIM1,
        [
            pltpu.VMEM(time_factor.shape, bf16),
            pltpu.VMEM((trials, components), bf16),
            pltpu.SemaphoreType.DMA((tri + 2,)),
        ],
    )(spike_counts, *[pltpu.with_memory_space_constraint(a, pltpu.HBM) for a in (time_factor, trial_factor)])
    parts = lax.all_to_all(part, "tri", 0, 0)
    copies, gram_time = call(
        neuron_solve,
        [array(tri, block, components), square],
        "neuron_solve",
        [WHOLE] * 4,
        5,
        [pltpu.VMEM((tri * trials, components), bf16)] + work,
    )(parts, time_factor, held(projected), held(spikes))
    raw = lax.all_to_all(copies, "tri", 0, 0).reshape(rows, components)
    (gram_part,) = call(neuron_gram, [square], "neuron_gram", [WHOLE] * 3)(raw, held(projected), held(spikes))
    (packed,) = call(
        pack_gram, [array(half, components // half + PAD, components)], "pack_gram", [WHOLE] * 2
    )(gram_part, lax.ppermute(gram_part, "neu", swap))
    groups = [list(range(c, neu, 2)) for c in range(2)]
    grams = lax.all_to_all(packed, "neu", 0, 0, axis_index_groups=groups)
    new, flipped, trial_part = call(
        lambda *refs: trial_pass(neu * rows, *refs),
        [
            array(rows, components),
            array(components, rows),
            array(half * tri, trials + PAD, components),
        ],
        "trial_pass",
        [WHOLE] * 4,
        5,
        [pltpu.VMEM((rows, components), f32)],
    )(grams, raw, held(projected), held(spikes))
    groups = [[n * tri + t for n in range(c, neu, 2) for t in range(tri)] for c in range(2)]
    gathered = lax.all_to_all(trial_part, both, 0, 0, axis_index_groups=groups)
    (ours,) = call(trial_sum, [array(tri * trials, components)], "trial_sum", [WHOLE] * 2)(gathered, held(spikes))
    theirs = lax.ppermute(ours, "neu", swap)
    inverse_two, gram_neuron = call(
        lambda *refs: second_system(neu * rows, *refs), [square, square], "second_system", [WHOLE] * 3, 4, work
    )(gram_time, gathered, held(spikes))
    neuron_new, trial_new, trial_table, time_part = call(
        time_pass,
        [
            array(rows, components),
            array(trials, components),
            array(tri * trials, components),
            array(components, bins),
        ],
        "time_pass",
        [WHOLE] * 6,
        5,
        [
            pltpu.VMEM((tri * trials, components), f32),
            pltpu.SemaphoreType.DMA((3,)),
        ],
        [in_hbm] * 3 + [WHOLE],
    )(ours, theirs, inverse_two, flipped, held(spikes), held(new))
    pieces = lax.all_to_all(time_part.reshape(neu * tri, components // (neu * tri), bins), both, 0, 0)
    (inverse_three,) = call(third_system, [square], "third_system", [WHOLE] * 2, 4, work)(gram_neuron, trial_table)
    piece = jnp.sum(pieces, axis=0, keepdims=True)
    mttkrp_time = lax.all_to_all(jnp.broadcast_to(piece, pieces.shape), both, 0, 0).reshape(components, bins)
    time_new, weights = call(time_solve, [array(bins, components), array(1, components)], "time_solve", [WHOLE] * 2)(
        mttkrp_time, inverse_three
    )
    return neuron_new, trial_new, time_new, weights[0]


def solution(mesh):
    return jax.shard_map(
        body,
        mesh=mesh,
        in_specs=(P("tri", "neu", None), P(), P("tri", None)),
        out_specs=(P("neu", None), P("tri", None), P(), P()),
        check_vma=False,
    )
```

```python
import jax
import jax.numpy as jnp
from jax import lax
from jax.experimental import pallas as pl
from jax.experimental.pallas import tpu as pltpu
from jax.sharding import PartitionSpec as P

LIM1 = 12
f32 = jnp.float32
bf16 = jnp.bfloat16
highest = lax.Precision.HIGHEST
WHOLE = pl.BlockSpec(memory_space=pltpu.VMEM)
MIB = 1 << 20
AHEAD = 3
PAD = 8


def call(kernel, outs, name, in_specs, limit=4, scratch=(), out_specs=None):
    return pl.pallas_call(
        kernel,
        in_specs=in_specs,
        out_specs=out_specs or [WHOLE] * len(outs),
        out_shape=outs,
        scratch_shapes=scratch,
        compiler_params=pltpu.CompilerParams(vmem_limit_bytes=limit * MIB),
        name=name,
    )


def held(value):
    return pltpu.with_memory_space_constraint(value, pltpu.VMEM)


def array(*shape):
    return jax.ShapeDtypeStruct(shape, f32)


def dot(a, b, dims=((1,), (0,))):
    return lax.dot_general(a, b, (dims, ((), ())), precision=highest, preferred_element_type=f32)


def rough(a, b):
    return jnp.dot(a.astype(bf16), b.astype(bf16), preferred_element_type=f32)


def fine(a, b):
    a_upper, b_upper = a.astype(bf16).astype(f32), b.astype(bf16).astype(f32)
    return rough(a_upper, b_upper) + (rough(a_upper, b - b_upper) + rough(a - a_upper, b_upper))


def identity(n):
    rows = lax.broadcasted_iota(jnp.int32, (n, n), 0)
    columns = lax.broadcasted_iota(jnp.int32, (n, n), 1)
    return jnp.where(rows == columns, 1.0, 0.0).astype(f32)


def row_norm(matrix):
    return jnp.max(jnp.sum(jnp.abs(matrix), axis=1, keepdims=True))


def inverse(system, scaled_ref, approx_ref, error_ref):
    n = system.shape[0]
    eye = identity(n)
    diagonal = system * eye
    left = 1.0 / jnp.sqrt(jnp.sum(diagonal, axis=1, keepdims=True))
    right = 1.0 / jnp.sqrt(jnp.sum(diagonal, axis=0, keepdims=True))
    scaled = system * left * right
    bound = row_norm(scaled)
    step = jnp.where(bound < 1.98, 1.0, 1.96 / bound)
    error = eye - step * scaled
    scaled_ref[...] = scaled
    approx_ref[...] = step * (eye + error)
    near = bound < 1.9

    @pl.when(near)
    def _():
        approx_ref[...] = approx_ref[...] + rough(approx_ref[...], rough(error, error))

    @pl.when(jnp.logical_not(near))
    def _():
        squared = dot(error, error)
        error_ref[...] = squared

        def going(state):
            count, norm = state
            return (norm > 1e-2) & (count < 40)

        def square(state):
            error = error_ref[...]
            approx = approx_ref[...]
            approx_ref[...] = approx + dot(approx, error)
            error = dot(error, error)
            error_ref[...] = error
            return state[0] + 1, row_norm(error)

        lax.while_loop(going, square, (0, row_norm(squared)))

    def refining(state):
        count, norm = state
        return (norm > 5e-4) & (count < 12)

    def refine(state):
        approx = approx_ref[...]
        residual = eye - dot(scaled_ref[...], approx)
        approx_ref[...] = approx + fine(approx, residual)
        return state[0] + 1, row_norm(residual)

    lax.while_loop(refining, refine, (0, jnp.float32(1.0)))
    approx = approx_ref[...]
    return approx * left * right


def neuron_pass(spikes_hbm, time_hbm, trial_hbm, spikes_ref, projected_ref, part_ref, time_ref, trial_ref, sems):
    trials = projected_ref.shape[0]
    blocks, extended, _ = part_ref.shape
    rows = extended - trials
    small = [
        pltpu.make_async_copy(time_hbm, time_ref, sems.at[blocks]),
        pltpu.make_async_copy(trial_hbm, trial_ref, sems.at[blocks + 1]),
    ]
    for copy in small:
        copy.start()
    copies = []
    for b in range(blocks):
        span = pl.ds(b * rows, rows)
        copies.append(
            pltpu.make_async_copy(spikes_hbm.at[:, span, :], spikes_ref.at[:, span, :], sems.at[b])
        )
    for b in range(min(AHEAD, blocks)):
        copies[b].start()
    for copy in small:
        copy.wait()
    trial = trial_ref[...].astype(f32)
    for b in range(blocks):
        copies[b].wait()
        if b + AHEAD < blocks:
            copies[b + AHEAD].start()
        span = pl.ds(b * rows, rows)
        total = None
        for k in range(trials):
            projected = jnp.dot(spikes_ref[k, span, :], time_ref[...], preferred_element_type=f32)
            projected_ref[k, span, :] = projected
            term = projected * trial[k : k + 1, :]
            total = term if total is None else total + term
        part_ref[b, 0:rows, :] = total
        part_ref[b, rows:extended, :] = trial


def neuron_solve(parts_ref, time_ref, held_ref, kept_ref, copies_ref, gram_time_ref, trial_ref, *work):
    blocks, extended, _ = parts_ref.shape
    rows = copies_ref.shape[1]
    trials = extended - rows
    total = parts_ref[0, 0:rows, :]
    for b in range(1, blocks):
        total = total + parts_ref[b, 0:rows, :]
    for b in range(blocks):
        trial_ref[b * trials : (b + 1) * trials, :] = parts_ref[b, rows:extended, :].astype(bf16)
    across = (((0,), (0,)), ((), ()))
    gram_time = lax.dot_general(time_ref[...], time_ref[...], across, preferred_element_type=f32)
    gram_trial = lax.dot_general(trial_ref[...], trial_ref[...], across, preferred_element_type=f32)
    gram_time_ref[...] = gram_time
    raw = dot(total, inverse(gram_time * gram_trial, *work))
    for b in range(copies_ref.shape[0]):
        copies_ref[b] = raw


def pack_gram(ours_ref, theirs_ref, packed_ref):
    blocks, extended, components = packed_ref.shape
    rows = components // blocks
    gram = ours_ref[...] + theirs_ref[...]
    diagonal = jnp.sum(gram * identity(components), axis=0, keepdims=True)
    for d in range(blocks):
        packed_ref[d, 0:rows, :] = gram[d * rows : (d + 1) * rows, :]
        packed_ref[d, rows:extended, :] = jnp.broadcast_to(diagonal, (extended - rows, components))


def neuron_gram(raw_ref, held_ref, kept_ref, gram_ref):
    components = raw_ref.shape[1]
    raw = raw_ref[...]
    upper = raw.astype(bf16)
    lower = (raw - upper.astype(f32)).astype(bf16)
    split = jnp.concatenate([upper, lower], axis=1)
    full = lax.dot_general(split, split, (((0,), (0,)), ((), ())), preferred_element_type=f32)
    gram_ref[...] = (
        full[:components, :components]
        + (full[:components, components:] + full[components:, :components])
        + full[components:, components:]
    )


def trial_pass(count, grams_ref, ours_ref, theirs_ref, projected_ref, kept_ref, new_ref, flipped_ref, part_ref, half_ref):
    trials, rows, components = projected_ref.shape
    ring = lax.axis_size("tri") // 2
    gram = jnp.sum(grams_ref[...], axis=0)
    lines = grams_ref.shape[1] - PAD
    scale = jnp.sqrt(gram[lines : lines + 1, :] / count + 1e-06)
    share = lines // ring
    here = lax.axis_index("tri")
    first = lax.rem(here, ring) * share
    place = lax.broadcasted_iota(jnp.int32, (lines, components), 0)
    spot = lax.broadcasted_iota(jnp.int32, (PAD, components), 0)
    sent = jnp.zeros((PAD, components), f32)
    for i in range(share):
        line = jnp.sum(jnp.where(place == first + i, gram[0:lines, :], 0.0), axis=0, keepdims=True)
        sent = jnp.where(spot == i, line, sent)
    ratio = 1.0 / scale
    for side, raw_ref in enumerate((ours_ref, theirs_ref)):
        count_rows = raw_ref.shape[0]
        span = pl.ds(pl.multiple_of(lax.rem(here // ring + side, 2) * count_rows, count_rows), count_rows)
        new = raw_ref[...] * ratio
        new_ref[span, :] = new
        flipped_ref[:, span] = new.T
        half_ref[span, :] = new.astype(bf16).astype(f32)
    block = 64

    def step(b, totals):
        span = pl.ds(pl.multiple_of(b * block, block), block)
        half = half_ref[span, :]
        return [
            totals[k]
            + jnp.sum((projected_ref[k, span, :] * half).reshape(block // 8, 8, components), axis=0)
            for k in range(trials)
        ]

    totals = lax.fori_loop(0, rows // block, step, [jnp.zeros((8, components), f32)] * trials, unroll=2)
    part = jnp.concatenate([jnp.sum(total, axis=0, keepdims=True) for total in totals], axis=0)
    for d in range(part_ref.shape[0]):
        part_ref[d, 0:trials, :] = part
        part_ref[d, trials:, :] = sent


def trial_sum(gathered_ref, kept_ref, sum_ref):
    tri = lax.axis_size("tri")
    chips = gathered_ref.shape[0]
    trials = gathered_ref.shape[1] - PAD
    for t in range(tri):
        total = gathered_ref[t, 0:trials, :]
        for d in range(t + tri, chips, tri):
            total = total + gathered_ref[d, 0:trials, :]
        sum_ref[t * trials : (t + 1) * trials, :] = total


def second_system(count, gram_time_ref, gathered_ref, kept_ref, inverse_ref, gram_ref, *work):
    components = gram_ref.shape[0]
    chips = gathered_ref.shape[0]
    trials = gathered_ref.shape[1] - PAD
    share = components // chips
    for d in range(chips):
        gram_ref[d * share : (d + 1) * share, :] = gathered_ref[d, trials : trials + share, :]
    gram_raw = gram_ref[...]
    diagonal = gram_raw * identity(components)
    scale = jnp.sqrt(jnp.sum(diagonal, axis=0, keepdims=True) / count + 1e-06)
    scale_down = jnp.sqrt(jnp.sum(diagonal, axis=1, keepdims=True) / count + 1e-06)
    gram = gram_raw / (scale * scale_down)
    gram_ref[...] = gram
    inverse_ref[...] = inverse(gram_time_ref[...] * gram, *work)


def time_pass(
    ours_ref, theirs_ref, inverse_ref, flipped_ref, spikes_ref, new_ref,
    new_hbm, trial_hbm, table_hbm, part_ref, table_ref, sems,
):
    new_copy = pltpu.make_async_copy(new_ref, new_hbm, sems.at[0])
    new_copy.start()
    trials, rows, bins = spikes_ref.shape
    components = inverse_ref.shape[0]
    raw = dot(ours_ref[...] + theirs_ref[...], inverse_ref[...])
    scale = jnp.sqrt(jnp.sum(raw * raw, axis=0, keepdims=True) / raw.shape[0] + 1e-06)
    table_ref[...] = raw / scale
    span = pl.ds(pl.multiple_of(lax.axis_index("tri") * trials, trials), trials)
    copies = [
        pltpu.make_async_copy(table_ref.at[span, :], trial_hbm, sems.at[1]),
        pltpu.make_async_copy(table_ref, table_hbm, sems.at[2]),
    ]
    for copy in copies:
        copy.start()
    columns = table_ref[span, :].T
    total = None
    for k in range(trials):
        khatri_rao = (flipped_ref[...] * columns[:, k : k + 1]).astype(bf16)
        term = jnp.dot(khatri_rao, spikes_ref[k], preferred_element_type=f32)
        total = term if total is None else total + term
    part_ref[...] = total
    for copy in [new_copy] + copies:
        copy.wait()


def third_system(gram_neuron_ref, table_ref, inverse_ref, *work):
    table = table_ref[...]
    inverse_ref[...] = inverse(gram_neuron_ref[...] * dot(table, table, ((0,), (0,))), *work)


def time_solve(mttkrp_ref, inverse_ref, time_ref, weights_ref):
    raw = dot(inverse_ref[...], mttkrp_ref[...]).T
    weights = jnp.sqrt(jnp.mean(raw * raw, axis=0, keepdims=True) + 1e-06)
    weights_ref[...] = weights
    time_ref[...] = raw / weights


def body(spike_counts, time_factor, trial_factor):
    trials, rows, bins = spike_counts.shape
    components = time_factor.shape[1]
    neu, tri = lax.axis_size("neu"), lax.axis_size("tri")
    block = rows // tri
    half = neu // 2
    both = ("neu", "tri")
    ring = tri // 2
    swap = [(i, i ^ 1) for i in range(neu)]
    in_hbm = pl.BlockSpec(memory_space=pltpu.HBM)

    square = array(components, components)
    work = [pltpu.VMEM((components, components), f32)] * 3

    spikes, projected, part = call(
        neuron_pass,
        [
            pltpu.VMEM(spike_counts.shape, bf16),
            pltpu.VMEM((trials, rows, components), f32),
            array(tri, block + trials, components),
        ],
        "neuron_pass",
        [in_hbm] * 3,
        LIM1,
        [
            pltpu.VMEM(time_factor.shape, bf16),
            pltpu.VMEM((trials, components), bf16),
            pltpu.SemaphoreType.DMA((tri + 2,)),
        ],
    )(spike_counts, *[pltpu.with_memory_space_constraint(a, pltpu.HBM) for a in (time_factor, trial_factor)])
    parts = lax.all_to_all(part, "tri", 0, 0)
    copies, gram_time = call(
        neuron_solve,
        [array(ring, block, components), square],
        "neuron_solve",
        [WHOLE] * 4,
        5,
        [pltpu.VMEM((tri * trials, components), bf16)] + work,
    )(parts, time_factor, held(projected), held(spikes))
    rings = [list(range(x * ring, (x + 1) * ring)) for x in range(2)]
    near = lax.all_to_all(copies, "tri", 0, 0, axis_index_groups=rings).reshape(rows // 2, components)
    far = lax.ppermute(near, "tri", [(t, (t + ring) % tri) for t in range(tri)])
    (gram_part,) = call(neuron_gram, [square], "neuron_gram", [WHOLE] * 3)(near, held(projected), held(spikes))
    (packed,) = call(
        pack_gram, [array(neu, components // neu + PAD, components)], "pack_gram", [WHOLE] * 2
    )(gram_part, lax.ppermute(gram_part, "neu", swap))
    groups = [
        [n * tri + x * ring + z for n in range(c, neu, 2) for x in range(2)] for c in range(2) for z in range(ring)
    ]
    grams = lax.all_to_all(packed, both, 0, 0, axis_index_groups=groups)
    new, flipped, trial_part = call(
        lambda *refs: trial_pass(neu * rows, *refs),
        [
            array(rows, components),
            array(components, rows),
            array(half * tri, trials + PAD, components),
        ],
        "trial_pass",
        [WHOLE] * 5,
        5,
        [pltpu.VMEM((rows, components), f32)],
    )(grams, near, far, held(projected), held(spikes))
    groups = [[n * tri + t for n in range(c, neu, 2) for t in range(tri)] for c in range(2)]
    gathered = lax.all_to_all(trial_part, both, 0, 0, axis_index_groups=groups)
    (ours,) = call(trial_sum, [array(tri * trials, components)], "trial_sum", [WHOLE] * 2)(gathered, held(spikes))
    theirs = lax.ppermute(ours, "neu", swap)
    inverse_two, gram_neuron = call(
        lambda *refs: second_system(neu * rows, *refs), [square, square], "second_system", [WHOLE] * 3, 4, work
    )(gram_time, gathered, held(spikes))
    neuron_new, trial_new, trial_table, time_part = call(
        time_pass,
        [
            array(rows, components),
            array(trials, components),
            array(tri * trials, components),
            array(components, bins),
        ],
        "time_pass",
        [WHOLE] * 6,
        5,
        [
            pltpu.VMEM((tri * trials, components), f32),
            pltpu.SemaphoreType.DMA((3,)),
        ],
        [in_hbm] * 3 + [WHOLE],
    )(ours, theirs, inverse_two, flipped, held(spikes), held(new))
    pieces = lax.all_to_all(time_part.reshape(neu * tri, components // (neu * tri), bins), both, 0, 0)
    (inverse_three,) = call(third_system, [square], "third_system", [WHOLE] * 2, 4, work)(gram_neuron, trial_table)
    piece = jnp.sum(pieces, axis=0, keepdims=True)
    mttkrp_time = lax.all_to_all(jnp.broadcast_to(piece, pieces.shape), both, 0, 0).reshape(components, bins)
    time_new, weights = call(time_solve, [array(bins, components), array(1, components)], "time_solve", [WHOLE] * 2)(
        mttkrp_time, inverse_three
    )
    return neuron_new, trial_new, time_new, weights[0]


def solution(mesh):
    return jax.shard_map(
        body,
        mesh=mesh,
        in_specs=(P("tri", "neu", None), P(), P("tri", None)),
        out_specs=(P("neu", None), P("tri", None), P(), P()),
        check_vma=False,
    )
```

```python
import jax
import jax.numpy as jnp
from jax import lax
from jax.experimental import pallas as pl
from jax.experimental.pallas import tpu as pltpu
from jax.sharding import PartitionSpec as P

LIM1 = 12
f32 = jnp.float32
bf16 = jnp.bfloat16
highest = lax.Precision.HIGHEST
WHOLE = pl.BlockSpec(memory_space=pltpu.VMEM)
MIB = 1 << 20
AHEAD = 3
PAD = 8


def call(kernel, outs, name, in_specs, limit=4, scratch=(), out_specs=None):
    return pl.pallas_call(
        kernel,
        in_specs=in_specs,
        out_specs=out_specs or [WHOLE] * len(outs),
        out_shape=outs,
        scratch_shapes=scratch,
        compiler_params=pltpu.CompilerParams(vmem_limit_bytes=limit * MIB),
        name=name,
    )


def held(value):
    return pltpu.with_memory_space_constraint(value, pltpu.VMEM)


def array(*shape):
    return jax.ShapeDtypeStruct(shape, f32)


def dot(a, b, dims=((1,), (0,))):
    return lax.dot_general(a, b, (dims, ((), ())), precision=highest, preferred_element_type=f32)


def rough(a, b):
    return jnp.dot(a.astype(bf16), b.astype(bf16), preferred_element_type=f32)


def fine(a, b):
    a_upper, b_upper = a.astype(bf16).astype(f32), b.astype(bf16).astype(f32)
    return rough(a_upper, b_upper) + (rough(a_upper, b - b_upper) + rough(a - a_upper, b_upper))


def identity(n):
    rows = lax.broadcasted_iota(jnp.int32, (n, n), 0)
    columns = lax.broadcasted_iota(jnp.int32, (n, n), 1)
    return jnp.where(rows == columns, 1.0, 0.0).astype(f32)


def row_norm(matrix):
    return jnp.max(jnp.sum(jnp.abs(matrix), axis=1, keepdims=True))


def inverse(system, scaled_ref, approx_ref, error_ref):
    n = system.shape[0]
    eye = identity(n)
    diagonal = system * eye
    left = 1.0 / jnp.sqrt(jnp.sum(diagonal, axis=1, keepdims=True))
    right = 1.0 / jnp.sqrt(jnp.sum(diagonal, axis=0, keepdims=True))
    scaled = system * left * right
    bound = row_norm(scaled)
    step = jnp.where(bound < 1.98, 1.0, 1.96 / bound)
    error = eye - step * scaled
    scaled_ref[...] = scaled
    approx_ref[...] = step * (eye + error)
    near = bound < 1.9

    @pl.when(near)
    def _():
        approx_ref[...] = approx_ref[...] + rough(approx_ref[...], rough(error, error))

    @pl.when(jnp.logical_not(near))
    def _():
        squared = dot(error, error)
        error_ref[...] = squared

        def going(state):
            count, norm = state
            return (norm > 1e-2) & (count < 40)

        def square(state):
            error = error_ref[...]
            approx = approx_ref[...]
            approx_ref[...] = approx + dot(approx, error)
            error = dot(error, error)
            error_ref[...] = error
            return state[0] + 1, row_norm(error)

        lax.while_loop(going, square, (0, row_norm(squared)))

    def refining(state):
        count, norm = state
        return (norm > 5e-4) & (count < 12)

    def refine(state):
        approx = approx_ref[...]
        residual = eye - dot(scaled_ref[...], approx)
        approx_ref[...] = approx + fine(approx, residual)
        return state[0] + 1, row_norm(residual)

    lax.while_loop(refining, refine, (0, jnp.float32(1.0)))
    approx = approx_ref[...]
    return approx * left * right


def neuron_pass(
    far, spikes_hbm, time_hbm, trial_hbm, *refs
):
    if not far:
        refs = refs[2:]
    spikes_ref, projected_ref, *part_refs, time_ref, trial_ref, sems = refs
    trials, total_rows, _ = projected_ref.shape
    ring = lax.axis_size("tri") // 2
    rows = total_rows // ring
    half, here = lax.axis_index("tri") // ring, lax.rem(lax.axis_index("tri"), ring)
    first = (lax.rem(half + 1, 2) if far else half) * total_rows
    small = [
        pltpu.make_async_copy(time_hbm, time_ref, sems.at[ring]),
        pltpu.make_async_copy(trial_hbm, trial_ref, sems.at[ring + 1]),
    ]
    for copy in small:
        copy.start()
    spans, copies = [], []
    for b in range(ring):
        place = lax.rem(here + b, ring) * rows
        span = pl.ds(pl.multiple_of(place, rows), rows)
        source = pl.ds(pl.multiple_of(first + place, rows), rows)
        spans.append(span)
        copies.append(
            pltpu.make_async_copy(spikes_hbm.at[:, source, :], spikes_ref.at[:, span, :], sems.at[b])
        )
    for copy in copies[:AHEAD]:
        copy.start()
    for copy in small:
        copy.wait()
    trial = trial_ref[...].astype(f32)
    for b in range(ring):
        copies[b].wait()
        if b + AHEAD < ring:
            copies[b + AHEAD].start()
        total = None
        for k in range(trials):
            projected = jnp.dot(spikes_ref[k, spans[b], :], time_ref[...], preferred_element_type=f32)
            projected_ref[k, spans[b], :] = projected
            term = projected * trial[k : k + 1, :]
            total = term if total is None else total + term
        part_ref = part_refs[b]
        part_ref[0:rows, :] = total
        part_ref[rows : rows + trials, :] = trial


def neuron_solve(*refs):
    blocks = lax.axis_size("tri")
    parts, refs = refs[:blocks], refs[blocks:]
    time_ref, *_, copies_ref, gram_time_ref, trial_ref, scaled_ref, approx_ref, error_ref = refs
    work = scaled_ref, approx_ref, error_ref
    extended, rows = parts[0].shape[0], copies_ref.shape[1]
    trials = extended - rows
    total = parts[0][0:rows, :]
    for part in parts[1:]:
        total = total + part[0:rows, :]
    for b, part in enumerate(parts):
        trial_ref[b * trials : (b + 1) * trials, :] = part[rows:extended, :].astype(bf16)
    across = (((0,), (0,)), ((), ()))
    gram_time = lax.dot_general(time_ref[...], time_ref[...], across, preferred_element_type=f32)
    gram_trial = lax.dot_general(trial_ref[...], trial_ref[...], across, preferred_element_type=f32)
    gram_time_ref[...] = gram_time
    raw = dot(total, inverse(gram_time * gram_trial, *work))
    for b in range(copies_ref.shape[0]):
        copies_ref[b] = raw


def pack_gram(ours_ref, theirs_ref, packed_ref):
    blocks, extended, components = packed_ref.shape
    rows = components // blocks
    gram = ours_ref[...] + theirs_ref[...]
    diagonal = jnp.sum(gram * identity(components), axis=0, keepdims=True)
    for d in range(blocks):
        packed_ref[d, 0:rows, :] = gram[d * rows : (d + 1) * rows, :]
        packed_ref[d, rows:extended, :] = jnp.broadcast_to(diagonal, (extended - rows, components))


def neuron_gram(raw_ref, *refs):
    gram_ref = refs[-1]
    components = raw_ref.shape[1]
    raw = raw_ref[...]
    upper = raw.astype(bf16)
    lower = (raw - upper.astype(f32)).astype(bf16)
    split = jnp.concatenate([upper, lower], axis=1)
    full = lax.dot_general(split, split, (((0,), (0,)), ((), ())), preferred_element_type=f32)
    gram_ref[...] = (
        full[:components, :components]
        + (full[:components, components:] + full[components:, :components])
        + full[components:, components:]
    )


def trial_pass(count, grams_ref, ours_ref, theirs_ref, near_ref, far_ref, *refs):
    *_, new_ref, flipped_ref, part_ref, half_ref = refs
    trials, rows, components = near_ref.shape
    ring = lax.axis_size("tri") // 2
    gram = jnp.sum(grams_ref[...], axis=0)
    lines = grams_ref.shape[1] - PAD
    scale = jnp.sqrt(gram[lines : lines + 1, :] / count + 1e-06)
    share = lines // ring
    here = lax.axis_index("tri")
    first = lax.rem(here, ring) * share
    place = lax.broadcasted_iota(jnp.int32, (lines, components), 0)
    spot = lax.broadcasted_iota(jnp.int32, (PAD, components), 0)
    sent = jnp.zeros((PAD, components), f32)
    for i in range(share):
        line = jnp.sum(jnp.where(place == first + i, gram[0:lines, :], 0.0), axis=0, keepdims=True)
        sent = jnp.where(spot == i, line, sent)
    ratio = 1.0 / scale
    for side, raw_ref in enumerate((ours_ref, theirs_ref)):
        span = slice(side * rows, (side + 1) * rows)
        new = raw_ref[...] * ratio
        new_ref[span, :] = new
        flipped_ref[:, span] = new.T
        half_ref[span, :] = new.astype(bf16).astype(f32)
    block = 64
    totals = [jnp.zeros((8, components), f32)] * trials
    for side, projected_ref in enumerate((near_ref, far_ref)):

        def step(b, totals):
            span = pl.ds(pl.multiple_of(b * block, block), block)
            half = half_ref[pl.ds(pl.multiple_of(side * rows + b * block, block), block), :]
            return [
                totals[k]
                + jnp.sum((projected_ref[k, span, :] * half).reshape(block // 8, 8, components), axis=0)
                for k in range(trials)
            ]

        totals = lax.fori_loop(0, rows // block, step, totals, unroll=2)
    part = jnp.concatenate([jnp.sum(total, axis=0, keepdims=True) for total in totals], axis=0)
    for d in range(part_ref.shape[0]):
        part_ref[d, 0:trials, :] = part
        part_ref[d, trials:, :] = sent


def trial_sum(gathered_ref, *refs):
    sum_ref = refs[-1]
    tri = lax.axis_size("tri")
    chips = gathered_ref.shape[0]
    trials = gathered_ref.shape[1] - PAD
    for t in range(tri):
        total = gathered_ref[t, 0:trials, :]
        for d in range(t + tri, chips, tri):
            total = total + gathered_ref[d, 0:trials, :]
        sum_ref[t * trials : (t + 1) * trials, :] = total


def second_system(count, gram_time_ref, gathered_ref, kept_ref, held_ref, inverse_ref, gram_ref, *work):
    components = gram_ref.shape[0]
    chips = gathered_ref.shape[0]
    trials = gathered_ref.shape[1] - PAD
    share = components // chips
    for d in range(chips):
        gram_ref[d * share : (d + 1) * share, :] = gathered_ref[d, trials : trials + share, :]
    gram_raw = gram_ref[...]
    diagonal = gram_raw * identity(components)
    scale = jnp.sqrt(jnp.sum(diagonal, axis=0, keepdims=True) / count + 1e-06)
    scale_down = jnp.sqrt(jnp.sum(diagonal, axis=1, keepdims=True) / count + 1e-06)
    gram = gram_raw / (scale * scale_down)
    gram_ref[...] = gram
    inverse_ref[...] = inverse(gram_time_ref[...] * gram, *work)


def time_pass(
    ours_ref, theirs_ref, inverse_ref, flipped_ref, near_ref, far_ref, new_ref,
    new_hbm, trial_hbm, table_hbm, part_ref, table_ref, sems,
):
    trials, rows, bins = near_ref.shape
    tri = lax.axis_size("tri")
    half = lax.axis_index("tri") // (tri // 2)
    moves = [
        pltpu.make_async_copy(
            new_ref.at[side * rows : (side + 1) * rows, :],
            new_hbm.at[pl.ds(pl.multiple_of(lax.rem(half + side, 2) * rows, rows), rows), :],
            sems.at[2 + side],
        )
        for side in range(2)
    ]
    for move in moves:
        move.start()
    components = inverse_ref.shape[0]
    raw = dot(ours_ref[...] + theirs_ref[...], inverse_ref[...])
    scale = jnp.sqrt(jnp.sum(raw * raw, axis=0, keepdims=True) / raw.shape[0] + 1e-06)
    table_ref[...] = raw / scale
    span = pl.ds(pl.multiple_of(lax.axis_index("tri") * trials, trials), trials)
    copies = [
        pltpu.make_async_copy(table_ref.at[span, :], trial_hbm, sems.at[0]),
        pltpu.make_async_copy(table_ref, table_hbm, sems.at[1]),
    ]
    for copy in copies:
        copy.start()
    columns = table_ref[span, :].T
    total = None
    for k in range(trials):
        khatri_rao = (flipped_ref[...] * columns[:, k : k + 1]).astype(bf16)
        for side, spikes_ref in enumerate((near_ref, far_ref)):
            piece = khatri_rao[:, side * rows : (side + 1) * rows]
            term = jnp.dot(piece, spikes_ref[k], preferred_element_type=f32)
            total = term if total is None else total + term
    part_ref[...] = total
    for copy in moves + copies:
        copy.wait()


def third_system(gram_neuron_ref, table_ref, inverse_ref, *work):
    table = table_ref[...]
    inverse_ref[...] = inverse(gram_neuron_ref[...] * dot(table, table, ((0,), (0,))), *work)


def time_solve(mttkrp_ref, inverse_ref, time_ref, weights_ref):
    raw = dot(inverse_ref[...], mttkrp_ref[...]).T
    weights = jnp.sqrt(jnp.mean(raw * raw, axis=0, keepdims=True) + 1e-06)
    weights_ref[...] = weights
    time_ref[...] = raw / weights


def body(spike_counts, time_factor, trial_factor):
    trials, rows, bins = spike_counts.shape
    components = time_factor.shape[1]
    neu, tri = lax.axis_size("neu"), lax.axis_size("tri")
    block = rows // tri
    half = neu // 2
    both = ("neu", "tri")
    ring = tri // 2
    swap = [(i, i ^ 1) for i in range(neu)]
    in_hbm = pl.BlockSpec(memory_space=pltpu.HBM)

    square = array(components, components)
    work = [pltpu.VMEM((components, components), f32)] * 3

    rings = [list(range(x * ring, (x + 1) * ring)) for x in range(2)]
    fetched = [pltpu.with_memory_space_constraint(a, pltpu.HBM) for a in (spike_counts, time_factor, trial_factor)]

    def first_pass(far, parts, *before):
        return call(
            lambda *refs: neuron_pass(far, *refs),
            [
                pltpu.VMEM((trials, rows // 2, bins), bf16),
                pltpu.VMEM((trials, rows // 2, components), f32),
            ]
            + parts,
            "far_pass" if far else "near_pass",
            [in_hbm] * 3 + [WHOLE] * len(before),
            LIM1,
            [
                pltpu.VMEM(time_factor.shape, bf16),
                pltpu.VMEM((trials, components), bf16),
                pltpu.SemaphoreType.DMA((ring + 2,)),
            ],
        )(*fetched, *before)

    def pass_on(value, x, z):
        pairs = [(t, (t // ring + x) % 2 * ring + (t % ring + z) % ring) for t in range(tri)]
        return lax.ppermute(value, "tri", pairs)

    pieces = [array(block + trials, components)] * ring
    spikes_far, projected_far, *far = first_pass(True, pieces)
    received = [pass_on(far[k], 1, k) for k in range(ring)]
    spikes_near, projected_near, *near = first_pass(False, pieces, held(spikes_far), held(projected_far))
    received += [near[0]] + [pass_on(near[k], 0, k) for k in range(1, ring)]
    spikes = [held(spikes_near), held(spikes_far)]
    projected = [held(projected_near), held(projected_far)]
    copies, gram_time = call(
        neuron_solve,
        [array(ring, block, components), square],
        "neuron_solve",
        [WHOLE] * (tri + 5),
        5,
        [pltpu.VMEM((tri * trials, components), bf16)] + work,
    )(*received, time_factor, *projected, *spikes)
    near = lax.all_to_all(copies, "tri", 0, 0, axis_index_groups=rings).reshape(rows // 2, components)
    far = lax.ppermute(near, "tri", [(t, (t + ring) % tri) for t in range(tri)])
    (gram_part,) = call(neuron_gram, [square], "neuron_gram", [WHOLE] * 5)(near, *projected, *spikes)
    (packed,) = call(
        pack_gram, [array(neu, components // neu + PAD, components)], "pack_gram", [WHOLE] * 2
    )(gram_part, lax.ppermute(gram_part, "neu", swap))
    groups = [
        [n * tri + x * ring + z for n in range(c, neu, 2) for x in range(2)] for c in range(2) for z in range(ring)
    ]
    grams = lax.all_to_all(packed, both, 0, 0, axis_index_groups=groups)
    new, flipped, trial_part = call(
        lambda *refs: trial_pass(neu * rows, *refs),
        [
            array(rows, components),
            array(components, rows),
            array(half * tri, trials + PAD, components),
        ],
        "trial_pass",
        [WHOLE] * 7,
        5,
        [pltpu.VMEM((rows, components), f32)],
    )(grams, near, far, *projected, *spikes)
    groups = [[n * tri + t for n in range(c, neu, 2) for t in range(tri)] for c in range(2)]
    gathered = lax.all_to_all(trial_part, both, 0, 0, axis_index_groups=groups)
    (ours,) = call(trial_sum, [array(tri * trials, components)], "trial_sum", [WHOLE] * 3)(gathered, *spikes)
    theirs = lax.ppermute(ours, "neu", swap)
    inverse_two, gram_neuron = call(
        lambda *refs: second_system(neu * rows, *refs), [square, square], "second_system", [WHOLE] * 4, 4, work
    )(gram_time, gathered, *spikes)
    neuron_new, trial_new, trial_table, time_part = call(
        time_pass,
        [
            array(rows, components),
            array(trials, components),
            array(tri * trials, components),
            array(components, bins),
        ],
        "time_pass",
        [WHOLE] * 7,
        5,
        [
            pltpu.VMEM((tri * trials, components), f32),
            pltpu.SemaphoreType.DMA((4,)),
        ],
        [in_hbm] * 3 + [WHOLE],
    )(ours, theirs, inverse_two, flipped, *spikes, held(new))
    pieces = lax.all_to_all(time_part.reshape(neu * tri, components // (neu * tri), bins), both, 0, 0)
    (inverse_three,) = call(third_system, [square], "third_system", [WHOLE] * 2, 4, work)(gram_neuron, trial_table)
    piece = jnp.sum(pieces, axis=0, keepdims=True)
    mttkrp_time = lax.all_to_all(jnp.broadcast_to(piece, pieces.shape), both, 0, 0).reshape(components, bins)
    time_new, weights = call(time_solve, [array(bins, components), array(1, components)], "time_solve", [WHOLE] * 2)(
        mttkrp_time, inverse_three
    )
    return neuron_new, trial_new, time_new, weights[0]


def solution(mesh):
    return jax.shard_map(
        body,
        mesh=mesh,
        in_specs=(P("tri", "neu", None), P(), P("tri", None)),
        out_specs=(P("neu", None), P("tri", None), P(), P()),
        check_vma=False,
    )
```

```python
import jax
import jax.numpy as jnp
from jax import lax
from jax.experimental import pallas as pl
from jax.experimental.pallas import tpu as pltpu
from jax.sharding import PartitionSpec as P

LIM1 = 12
f32 = jnp.float32
bf16 = jnp.bfloat16
highest = lax.Precision.HIGHEST
WHOLE = pl.BlockSpec(memory_space=pltpu.VMEM)
MIB = 1 << 20
AHEAD = 4
PAD = 8


def call(kernel, outs, name, in_specs, limit=4, scratch=(), out_specs=None):
    return pl.pallas_call(
        kernel,
        in_specs=in_specs,
        out_specs=out_specs or [WHOLE] * len(outs),
        out_shape=outs,
        scratch_shapes=scratch,
        compiler_params=pltpu.CompilerParams(vmem_limit_bytes=limit * MIB),
        name=name,
    )


def held(value):
    return pltpu.with_memory_space_constraint(value, pltpu.VMEM)


def array(*shape):
    return jax.ShapeDtypeStruct(shape, f32)


def dot(a, b, dims=((1,), (0,))):
    return lax.dot_general(a, b, (dims, ((), ())), precision=highest, preferred_element_type=f32)


def rough(a, b):
    return jnp.dot(a.astype(bf16), b.astype(bf16), preferred_element_type=f32)


def fine(a, b):
    a_upper, b_upper = a.astype(bf16).astype(f32), b.astype(bf16).astype(f32)
    return rough(a_upper, b_upper) + (rough(a_upper, b - b_upper) + rough(a - a_upper, b_upper))


def identity(n):
    rows = lax.broadcasted_iota(jnp.int32, (n, n), 0)
    columns = lax.broadcasted_iota(jnp.int32, (n, n), 1)
    return jnp.where(rows == columns, 1.0, 0.0).astype(f32)


def row_norm(matrix):
    return jnp.max(jnp.sum(jnp.abs(matrix), axis=1, keepdims=True))


def inverse(system, scaled_ref, approx_ref, error_ref):
    n = system.shape[0]
    eye = identity(n)
    diagonal = system * eye
    left = 1.0 / jnp.sqrt(jnp.sum(diagonal, axis=1, keepdims=True))
    right = 1.0 / jnp.sqrt(jnp.sum(diagonal, axis=0, keepdims=True))
    scaled = system * left * right
    bound = row_norm(scaled)
    step = jnp.where(bound < 1.98, 1.0, 1.96 / bound)
    error = eye - step * scaled
    scaled_ref[...] = scaled
    approx_ref[...] = step * (eye + error)
    near = bound < 1.9

    @pl.when(near)
    def _():
        approx_ref[...] = approx_ref[...] + rough(approx_ref[...], rough(error, error))

    @pl.when(jnp.logical_not(near))
    def _():
        squared = dot(error, error)
        error_ref[...] = squared

        def going(state):
            count, norm = state
            return (norm > 1e-2) & (count < 40)

        def square(state):
            error = error_ref[...]
            approx = approx_ref[...]
            approx_ref[...] = approx + dot(approx, error)
            error = dot(error, error)
            error_ref[...] = error
            return state[0] + 1, row_norm(error)

        lax.while_loop(going, square, (0, row_norm(squared)))

    def refining(state):
        count, norm = state
        return (norm > 5e-4) & (count < 12)

    def refine(state):
        approx = approx_ref[...]
        residual = eye - dot(scaled_ref[...], approx)
        approx_ref[...] = approx + fine(approx, residual)
        return state[0] + 1, row_norm(residual)

    lax.while_loop(refining, refine, (0, jnp.float32(1.0)))
    approx = approx_ref[...]
    return approx * left * right


def neuron_pass(
    far, spikes_hbm, time_hbm, trial_hbm, *refs
):
    if not far:
        refs = refs[2:]
    spikes_ref, projected_ref, *part_refs, time_ref, trial_ref, sems = refs
    trials, total_rows, _ = projected_ref.shape
    ring = lax.axis_size("tri") // 2
    rows = total_rows // ring
    half, here = lax.axis_index("tri") // ring, lax.rem(lax.axis_index("tri"), ring)
    first = (lax.rem(half + 1, 2) if far else half) * total_rows
    small = [
        pltpu.make_async_copy(time_hbm, time_ref, sems.at[ring]),
        pltpu.make_async_copy(trial_hbm, trial_ref, sems.at[ring + 1]),
    ]
    for copy in small:
        copy.start()
    spans, copies = [], []
    for b in range(ring):
        place = lax.rem(here + b, ring) * rows
        span = pl.ds(pl.multiple_of(place, rows), rows)
        source = pl.ds(pl.multiple_of(first + place, rows), rows)
        spans.append(span)
        copies.append(
            pltpu.make_async_copy(spikes_hbm.at[:, source, :], spikes_ref.at[:, span, :], sems.at[b])
        )
    for copy in copies[:AHEAD]:
        copy.start()
    for copy in small:
        copy.wait()
    trial = trial_ref[...].astype(f32)
    for b in range(ring):
        copies[b].wait()
        if b + AHEAD < ring:
            copies[b + AHEAD].start()
        total = None
        for k in range(trials):
            projected = jnp.dot(spikes_ref[k, spans[b], :], time_ref[...], preferred_element_type=f32)
            projected_ref[k, spans[b], :] = projected
            term = projected * trial[k : k + 1, :]
            total = term if total is None else total + term
        part_ref = part_refs[b]
        part_ref[0:rows, :] = total
        part_ref[rows : rows + trials, :] = trial


def neuron_solve(*refs):
    blocks = lax.axis_size("tri")
    parts, refs = refs[:blocks], refs[blocks:]
    time_ref, *_, copies_ref, gram_time_ref, trial_ref, scaled_ref, approx_ref, error_ref = refs
    work = scaled_ref, approx_ref, error_ref
    extended, rows = parts[0].shape[0], copies_ref.shape[1]
    trials = extended - rows
    total = parts[0][0:rows, :]
    for part in parts[1:]:
        total = total + part[0:rows, :]
    for b, part in enumerate(parts):
        trial_ref[b * trials : (b + 1) * trials, :] = part[rows:extended, :].astype(bf16)
    across = (((0,), (0,)), ((), ()))
    gram_time = lax.dot_general(time_ref[...], time_ref[...], across, preferred_element_type=f32)
    gram_trial = lax.dot_general(trial_ref[...], trial_ref[...], across, preferred_element_type=f32)
    gram_time_ref[...] = gram_time
    raw = dot(total, inverse(gram_time * gram_trial, *work))
    for b in range(copies_ref.shape[0]):
        copies_ref[b] = raw


def pack_gram(ours_ref, theirs_ref, packed_ref):
    blocks, extended, components = packed_ref.shape
    rows = components // blocks
    gram = ours_ref[...] + theirs_ref[...]
    diagonal = jnp.sum(gram * identity(components), axis=0, keepdims=True)
    for d in range(blocks):
        packed_ref[d, 0:rows, :] = gram[d * rows : (d + 1) * rows, :]
        packed_ref[d, rows:extended, :] = jnp.broadcast_to(diagonal, (extended - rows, components))


def neuron_gram(raw_ref, *refs):
    gram_ref = refs[-1]
    components = raw_ref.shape[1]
    raw = raw_ref[...]
    upper = raw.astype(bf16)
    lower = (raw - upper.astype(f32)).astype(bf16)
    split = jnp.concatenate([upper, lower], axis=1)
    full = lax.dot_general(split, split, (((0,), (0,)), ((), ())), preferred_element_type=f32)
    gram_ref[...] = (
        full[:components, :components]
        + (full[:components, components:] + full[components:, :components])
        + full[components:, components:]
    )


def trial_pass(count, grams_ref, ours_ref, theirs_ref, near_ref, far_ref, *refs):
    *_, new_ref, flipped_ref, part_ref, half_ref = refs
    trials, rows, components = near_ref.shape
    ring = lax.axis_size("tri") // 2
    gram = jnp.sum(grams_ref[...], axis=0)
    lines = grams_ref.shape[1] - PAD
    scale = jnp.sqrt(gram[lines : lines + 1, :] / count + 1e-06)
    share = lines // ring
    here = lax.axis_index("tri")
    first = lax.rem(here, ring) * share
    place = lax.broadcasted_iota(jnp.int32, (lines, components), 0)
    spot = lax.broadcasted_iota(jnp.int32, (PAD, components), 0)
    sent = jnp.zeros((PAD, components), f32)
    for i in range(share):
        line = jnp.sum(jnp.where(place == first + i, gram[0:lines, :], 0.0), axis=0, keepdims=True)
        sent = jnp.where(spot == i, line, sent)
    ratio = 1.0 / scale
    for side, raw_ref in enumerate((ours_ref, theirs_ref)):
        span = slice(side * rows, (side + 1) * rows)
        new = raw_ref[...] * ratio
        new_ref[span, :] = new
        flipped_ref[:, span] = new.T
        half_ref[span, :] = new.astype(bf16).astype(f32)
    block = 64
    totals = [jnp.zeros((8, components), f32)] * trials
    for side, projected_ref in enumerate((near_ref, far_ref)):

        def step(b, totals):
            span = pl.ds(pl.multiple_of(b * block, block), block)
            half = half_ref[pl.ds(pl.multiple_of(side * rows + b * block, block), block), :]
            return [
                totals[k]
                + jnp.sum((projected_ref[k, span, :] * half).reshape(block // 8, 8, components), axis=0)
                for k in range(trials)
            ]

        totals = lax.fori_loop(0, rows // block, step, totals, unroll=2)
    part = jnp.concatenate([jnp.sum(total, axis=0, keepdims=True) for total in totals], axis=0)
    for d in range(part_ref.shape[0]):
        part_ref[d, 0:trials, :] = part
        part_ref[d, trials:, :] = sent


def trial_sum(gathered_ref, *refs):
    sum_ref = refs[-1]
    tri = lax.axis_size("tri")
    chips = gathered_ref.shape[0]
    trials = gathered_ref.shape[1] - PAD
    for t in range(tri):
        total = gathered_ref[t, 0:trials, :]
        for d in range(t + tri, chips, tri):
            total = total + gathered_ref[d, 0:trials, :]
        sum_ref[t * trials : (t + 1) * trials, :] = total


def second_system(count, gram_time_ref, gathered_ref, kept_ref, held_ref, inverse_ref, gram_ref, *work):
    components = gram_ref.shape[0]
    chips = gathered_ref.shape[0]
    trials = gathered_ref.shape[1] - PAD
    share = components // chips
    for d in range(chips):
        gram_ref[d * share : (d + 1) * share, :] = gathered_ref[d, trials : trials + share, :]
    gram_raw = gram_ref[...]
    diagonal = gram_raw * identity(components)
    scale = jnp.sqrt(jnp.sum(diagonal, axis=0, keepdims=True) / count + 1e-06)
    scale_down = jnp.sqrt(jnp.sum(diagonal, axis=1, keepdims=True) / count + 1e-06)
    gram = gram_raw / (scale * scale_down)
    gram_ref[...] = gram
    inverse_ref[...] = inverse(gram_time_ref[...] * gram, *work)


def time_pass(
    ours_ref, theirs_ref, inverse_ref, flipped_ref, near_ref, far_ref, new_ref,
    new_hbm, trial_hbm, table_hbm, part_ref, table_ref, sems,
):
    trials, rows, bins = near_ref.shape
    tri = lax.axis_size("tri")
    half = lax.axis_index("tri") // (tri // 2)
    moves = [
        pltpu.make_async_copy(
            new_ref.at[side * rows : (side + 1) * rows, :],
            new_hbm.at[pl.ds(pl.multiple_of(lax.rem(half + side, 2) * rows, rows), rows), :],
            sems.at[2 + side],
        )
        for side in range(2)
    ]
    for move in moves:
        move.start()
    components = inverse_ref.shape[0]
    raw = dot(ours_ref[...] + theirs_ref[...], inverse_ref[...])
    scale = jnp.sqrt(jnp.sum(raw * raw, axis=0, keepdims=True) / raw.shape[0] + 1e-06)
    table_ref[...] = raw / scale
    span = pl.ds(pl.multiple_of(lax.axis_index("tri") * trials, trials), trials)
    copies = [
        pltpu.make_async_copy(table_ref.at[span, :], trial_hbm, sems.at[0]),
        pltpu.make_async_copy(table_ref, table_hbm, sems.at[1]),
    ]
    for copy in copies:
        copy.start()
    columns = table_ref[span, :].T
    total = None
    for k in range(trials):
        khatri_rao = (flipped_ref[...] * columns[:, k : k + 1]).astype(bf16)
        for side, spikes_ref in enumerate((near_ref, far_ref)):
            piece = khatri_rao[:, side * rows : (side + 1) * rows]
            term = jnp.dot(piece, spikes_ref[k], preferred_element_type=f32)
            total = term if total is None else total + term
    part_ref[...] = total
    for copy in moves + copies:
        copy.wait()


def third_system(gram_neuron_ref, table_ref, inverse_ref, *work):
    table = table_ref[...]
    inverse_ref[...] = inverse(gram_neuron_ref[...] * dot(table, table, ((0,), (0,))), *work)


def time_solve(mttkrp_ref, inverse_ref, time_ref, weights_ref):
    raw = fine(inverse_ref[...], mttkrp_ref[...]).T
    weights = jnp.sqrt(jnp.mean(raw * raw, axis=0, keepdims=True) + 1e-06)
    weights_ref[...] = weights
    time_ref[...] = raw / weights


def body(spike_counts, time_factor, trial_factor):
    trials, rows, bins = spike_counts.shape
    components = time_factor.shape[1]
    neu, tri = lax.axis_size("neu"), lax.axis_size("tri")
    block = rows // tri
    half = neu // 2
    both = ("neu", "tri")
    ring = tri // 2
    swap = [(i, i ^ 1) for i in range(neu)]
    in_hbm = pl.BlockSpec(memory_space=pltpu.HBM)

    square = array(components, components)
    work = [pltpu.VMEM((components, components), f32)] * 3

    rings = [list(range(x * ring, (x + 1) * ring)) for x in range(2)]
    fetched = [pltpu.with_memory_space_constraint(a, pltpu.HBM) for a in (spike_counts, time_factor, trial_factor)]

    def first_pass(far, parts, *before):
        return call(
            lambda *refs: neuron_pass(far, *refs),
            [
                pltpu.VMEM((trials, rows // 2, bins), bf16),
                pltpu.VMEM((trials, rows // 2, components), f32),
            ]
            + parts,
            "far_pass" if far else "near_pass",
            [in_hbm] * 3 + [WHOLE] * len(before),
            LIM1,
            [
                pltpu.VMEM(time_factor.shape, bf16),
                pltpu.VMEM((trials, components), bf16),
                pltpu.SemaphoreType.DMA((ring + 2,)),
            ],
        )(*fetched, *before)

    def pass_on(value, x, z):
        pairs = [(t, (t // ring + x) % 2 * ring + (t % ring + z) % ring) for t in range(tri)]
        return lax.ppermute(value, "tri", pairs)

    pieces = [array(block + trials, components)] * ring
    spikes_far, projected_far, *far = first_pass(True, pieces)
    received = [pass_on(far[k], 1, k) for k in range(ring)]
    spikes_near, projected_near, *near = first_pass(False, pieces, held(spikes_far), held(projected_far))
    received += [near[0]] + [pass_on(near[k], 0, k) for k in range(1, ring)]
    spikes = [held(spikes_near), held(spikes_far)]
    projected = [held(projected_near), held(projected_far)]
    copies, gram_time = call(
        neuron_solve,
        [array(ring, block, components), square],
        "neuron_solve",
        [WHOLE] * (tri + 5),
        5,
        [pltpu.VMEM((tri * trials, components), bf16)] + work,
    )(*received, time_factor, *projected, *spikes)
    near = lax.all_to_all(copies, "tri", 0, 0, axis_index_groups=rings).reshape(rows // 2, components)
    far = lax.ppermute(near, "tri", [(t, (t + ring) % tri) for t in range(tri)])
    (gram_part,) = call(neuron_gram, [square], "neuron_gram", [WHOLE] * 5)(near, *projected, *spikes)
    (packed,) = call(
        pack_gram, [array(neu, components // neu + PAD, components)], "pack_gram", [WHOLE] * 2
    )(gram_part, lax.ppermute(gram_part, "neu", swap))
    groups = [
        [n * tri + x * ring + z for n in range(c, neu, 2) for x in range(2)] for c in range(2) for z in range(ring)
    ]
    grams = lax.all_to_all(packed, both, 0, 0, axis_index_groups=groups)
    new, flipped, trial_part = call(
        lambda *refs: trial_pass(neu * rows, *refs),
        [
            array(rows, components),
            array(components, rows),
            array(half * tri, trials + PAD, components),
        ],
        "trial_pass",
        [WHOLE] * 7,
        5,
        [pltpu.VMEM((rows, components), f32)],
    )(grams, near, far, *projected, *spikes)
    groups = [[n * tri + t for n in range(c, neu, 2) for t in range(tri)] for c in range(2)]
    gathered = lax.all_to_all(trial_part, both, 0, 0, axis_index_groups=groups)
    (ours,) = call(trial_sum, [array(tri * trials, components)], "trial_sum", [WHOLE] * 3)(gathered, *spikes)
    theirs = lax.ppermute(ours, "neu", swap)
    inverse_two, gram_neuron = call(
        lambda *refs: second_system(neu * rows, *refs), [square, square], "second_system", [WHOLE] * 4, 4, work
    )(gram_time, gathered, *spikes)
    neuron_new, trial_new, trial_table, time_part = call(
        time_pass,
        [
            array(rows, components),
            array(trials, components),
            array(tri * trials, components),
            array(components, bins),
        ],
        "time_pass",
        [WHOLE] * 7,
        5,
        [
            pltpu.VMEM((tri * trials, components), f32),
            pltpu.SemaphoreType.DMA((4,)),
        ],
        [in_hbm] * 3 + [WHOLE],
    )(ours, theirs, inverse_two, flipped, *spikes, held(new))
    pieces = lax.all_to_all(time_part.reshape(neu * tri, components // (neu * tri), bins), both, 0, 0)
    (inverse_three,) = call(third_system, [square], "third_system", [WHOLE] * 2, 4, work)(gram_neuron, trial_table)
    piece = jnp.sum(pieces, axis=0, keepdims=True)
    mttkrp_time = lax.all_to_all(jnp.broadcast_to(piece, pieces.shape), both, 0, 0).reshape(components, bins)
    time_new, weights = call(time_solve, [array(bins, components), array(1, components)], "time_solve", [WHOLE] * 2)(
        mttkrp_time, inverse_three
    )
    return neuron_new, trial_new, time_new, weights[0]


def solution(mesh):
    return jax.shard_map(
        body,
        mesh=mesh,
        in_specs=(P("tri", "neu", None), P(), P("tri", None)),
        out_specs=(P("neu", None), P("tri", None), P(), P()),
        check_vma=False,
    )
```
